32 devices in a mesh: dp: 8 (over z, y), seq: 4 (over x, core).
Axes of the slice: x: 2, y: 2, z: 4, core: 2. Of those that a mesh axis runs over, the one named last changes fastest.
Arguments:
- tokens: bfloat16 [32, 8, 196, 768], P('dp', 'seq'), may hold values from -6 to 6
- temporal_gain: bfloat16 [768], P(('dp', 'seq')), may hold values from 0.5 to 1.5
- temporal_biases: bfloat16 [3, 768], P(None, ('dp', 'seq')), may hold values from -1.1953125 to 1.1953125
- temporal_inproj: bfloat16 [768, 2304], P(('dp', 'seq')), may hold values from -0.21875 to 0.21875
- temporal_outproj: bfloat16 [768, 768], P(('dp', 'seq')), may hold values from -0.4375 to 0.4375
- temporal_linear: bfloat16 [768, 768], P(('dp', 'seq')), may hold values from -0.21875 to 0.21875
- spatial_gain: bfloat16 [768], P(('dp', 'seq')), may hold values from 0.5 to 1.5
- spatial_biases: bfloat16 [2, 768], P(None, ('dp', 'seq')), may hold values from -1.1953125 to 1.1953125
- spatial_inproj: bfloat16 [768, 2304], P(('dp', 'seq')), may hold values from -0.21875 to 0.21875
- spatial_outproj: bfloat16 [768, 768], P(('dp', 'seq')), may hold values from -1.75 to 1.75
- feed_gain: bfloat16 [768], P(('dp', 'seq')), may hold values from 0.5 to 1.5
- feed_biases: bfloat16 [2, 768], P(None, ('dp', 'seq')), may hold values from -1.1953125 to 1.1953125
- widen_weight: bfloat16 [768, 3072], P(('dp', 'seq')), may hold values from -0.21875 to 0.21875
- widen_bias: bfloat16 [3072], P(('dp', 'seq')), may hold values from -1.1953125 to 1.1953125
- narrow_weight: bfloat16 [3072, 768], P(('dp', 'seq')), may hold values from -0.109375 to 0.109375
- cotangent: bfloat16 [32, 8, 196, 768], P('dp', 'seq'), may hold values from -6 to 6
Outputs:
- output: bfloat16 [32, 8, 196, 768], P('dp', 'seq')
- grad_tokens: bfloat16 [32, 8, 196, 768], P('dp', 'seq')
- grad_temporal_gain: float32 [768], P(('dp', 'seq'))
- grad_temporal_biases: float32 [3, 768], P(None, ('dp', 'seq'))
- grad_temporal_inproj: float32 [768, 2304], P(('dp', 'seq'))
- grad_temporal_outproj: float32 [768, 768], P(('dp', 'seq'))
- grad_temporal_linear: float32 [768, 768], P(('dp', 'seq'))
- grad_spatial_gain: float32 [768], P(('dp', 'seq'))
- grad_spatial_biases: float32 [2, 768], P(None, ('dp', 'seq'))
- grad_spatial_inproj: float32 [768, 2304], P(('dp', 'seq'))
- grad_spatial_outproj: float32 [768, 768], P(('dp', 'seq'))
- grad_feed_gain: float32 [768], P(('dp', 'seq'))
- grad_feed_biases: float32 [2, 768], P(None, ('dp', 'seq'))
- grad_widen_weight: float32 [768, 3072], P(('dp', 'seq'))
- grad_widen_bias: float32 [3072], P(('dp', 'seq'))
- grad_narrow_weight: float32 [3072, 768], P(('dp', 'seq'))
The draws below stay inside these ranges and needn't reach their ends.
All inputs are finite; a program needn't handle non-finite values.
Results may differ from the reference program's by a relative error of at most 0.02.
Values may be sent and summed in bfloat16 or wider, within the bound.
No kernel may reach another device: no remote copies, remote signals or barrier semaphores. Data moves between devices by JAX's collectives and lax.ppermute only.
A program may use at most 320 MiB of HBM per device.

```python
import jax
import jax.numpy as jnp
from jax import lax

D = 768
HEADS = 12
HEAD_DIM = 64
FF = 3072
FRAMES = 8
PLACES = 196
CLIPS_DEV = 4
CLIPS = 32
N_DP = 8


def strengthened(values, own_key, source, target, shards_of, factor):
    def block_of(dim):
        return (jnp.arange(values.shape[dim]) // (values.shape[dim] // shards_of)).reshape((-1,) + (1,) * (values.ndim - 1 - dim))

    one_side = jax.random.permutation(own_key, shards_of)[block_of(target)]
    other_side = (block_of(target) + shards_of // 2) % shards_of
    return jnp.where((block_of(source) == one_side) | (block_of(source) == other_side), factor * values, values)


def level_of(key, dims, split, low, high):
    def one(axis_at, parts):
        heights = jax.random.uniform(jax.random.fold_in(jax.random.fold_in(key, 6), axis_at), (parts,), jnp.float32, low / len(split), high / len(split))
        return jnp.repeat(jnp.exp(heights), dims[axis_at] // parts).reshape((-1,) + (1,) * (len(dims) - axis_at - 1))

    gain = one(*split[0])
    for cut in split[1:]:
        gain = gain * one(*cut)
    return gain


def gaussian(rng, dims, deviation, bound, split=(), kind=jnp.bfloat16):
    entries = jax.random.normal(rng, dims, jnp.float32) * deviation
    if len(split) > 0:
        entries = level_of(rng, dims, split, -0.22, 0.18) * entries
    return jnp.clip(entries, min=-bound, max=bound).astype(kind)


def gaussian_with(key, shape, width, bound, pieces, heavy, dtype=jnp.bfloat16):
    values = width * jax.random.normal(key, shape, jnp.float32)
    if pieces:
        values = values * level_of(key, shape, pieces, -0.22, 0.18)
    return jnp.clip(strengthened(values, jax.random.fold_in(key, 3), *heavy), -bound, bound).astype(dtype)


def setup_inputs(seed: int = 0) -> dict:
    streams_of = jax.random.split(jax.random.key(seed), 17)
    return {
        "tokens": gaussian(streams_of[0], (CLIPS, FRAMES, PLACES, D), 1.0, 6.0, ((0, 8), (1, 4))),
        "temporal_gain": jnp.clip(1.0 + 0.1 * jax.random.normal(streams_of[1], (D,), jnp.float32), 0.5, 1.5).astype(jnp.bfloat16),
        "temporal_biases": gaussian(streams_of[2], (3, D), 0.2, 1.1953125, ((1, 32),)),
        "temporal_inproj": gaussian(streams_of[3], (D, 3 * D), D ** -0.5, 0.21875, ((0, 32),)),
        "temporal_outproj": gaussian(streams_of[4], (D, D), (D // 4) ** -0.5, 0.4375, ((0, 32),)),
        "temporal_linear": gaussian(streams_of[5], (D, D), D ** -0.5, 0.21875, ((0, 32),)),
        "spatial_gain": jnp.clip(1.0 + 0.1 * jax.random.normal(streams_of[6], (D,), jnp.float32), 0.5, 1.5).astype(jnp.bfloat16),
        "spatial_biases": gaussian(streams_of[7], (2, D), 0.2, 1.1953125, ((1, 32),)),
        "spatial_inproj": gaussian(streams_of[8], (D, 3 * D), D ** -0.5, 0.21875, ((0, 32),)),
        "spatial_outproj": gaussian(streams_of[9], (D, D), (D // 64) ** -0.5, 1.75, ((0, 32),)),
        "feed_gain": jnp.clip(1.0 + 0.1 * jax.random.normal(streams_of[10], (D,), jnp.float32), 0.5, 1.5).astype(jnp.bfloat16),
        "feed_biases": gaussian(streams_of[11], (2, D), 0.2, 1.1953125, ((1, 32),)),
        "widen_weight": gaussian(streams_of[12], (D, FF), D ** -0.5, 0.21875, ((0, 32),)),
        "widen_bias": gaussian(streams_of[13], (FF,), 0.2, 1.1953125, ((0, 32),)),
        "narrow_weight": gaussian(streams_of[14], (FF, D), FF ** -0.5, 0.109375, ((0, 32),)),
        "cotangent": gaussian_with(streams_of[15], (CLIPS, FRAMES, PLACES, D), 1.0, 6.0, ((0, 8), (1, 4)), (0, 3, 8, 2.0)),
    }


@jax.custom_vjp
def low(v):
    return lax.optimization_barrier(v.astype(jnp.bfloat16)).astype(jnp.float32)

@jax.custom_vjp
def low_back(v):
    return v

def low_keep(v):
    return (low(v), None)

def low_pass(kept, grad):
    return (grad,)

def back_keep(v):
    return (v, None)

def back_low(kept, grad):
    return (low(grad),)
low.defvjp(low_keep, low_pass)
low_back.defvjp(back_keep, back_low)

def round_both(values):
    return low_back(low(values))

def norm_rows(values, gain_row, bias_row):
    center = values - lax.optimization_barrier(jnp.mean(values, axis=-1, keepdims=True))
    spread = lax.optimization_barrier(jnp.mean(center * center, axis=-1, keepdims=True))
    return center * lax.rsqrt(spread + 1e-05) * gain_row + bias_row

def project(left_side, right_side):
    return jnp.einsum('...k,kn->...n', left_side, right_side, precision=lax.Precision.HIGHEST)

def attend(joined):
    seq_count, length = (joined.shape[0], joined.shape[1])
    parted = joined.reshape(seq_count, length, 3, HEADS, HEAD_DIM)
    query_heads, key_heads, value_heads = (parted[:, :, 0], parted[:, :, 1], parted[:, :, 2])
    raw_scores = jnp.einsum('blhd,bmhd->bhlm', query_heads, key_heads, precision=lax.Precision.HIGHEST)
    scores = low_back(raw_scores * HEAD_DIM ** (-0.5))
    shares = low(jax.nn.softmax(scores, axis=-1))
    mixture = jnp.einsum('bhlm,bmhd->blhd', shares, value_heads, precision=lax.Precision.HIGHEST)
    return round_both(mixture.reshape(seq_count, length, HEADS * HEAD_DIM))

def layer(parameters, clip_block):
    temporal_gain, temporal_biases, temporal_inproj, temporal_outproj, temporal_linear, spatial_gain, spatial_biases, spatial_inproj, spatial_outproj, feed_gain, feed_biases, widen_weight, widen_bias, narrow_weight = parameters
    clip_count = clip_block.shape[0]
    temporal_norm = round_both(norm_rows(clip_block, temporal_gain, temporal_biases[0]))
    temporal_joined = round_both(project(temporal_norm, temporal_inproj))
    temporal_seqs = jnp.transpose(temporal_joined, (0, 2, 1, 3)).reshape(clip_count * PLACES, FRAMES, 3 * D)
    temporal_mixed = attend(temporal_seqs).reshape(clip_count, PLACES, FRAMES, D)
    temporal_mixed = jnp.transpose(temporal_mixed, (0, 2, 1, 3))
    temporal_proj = round_both(project(temporal_mixed, temporal_outproj) + temporal_biases[1])
    temporal_branch = round_both(project(temporal_proj, temporal_linear) + temporal_biases[2])
    after_time = clip_block + temporal_branch
    spatial_norm = low(norm_rows(after_time, spatial_gain, spatial_biases[0]))
    spatial_joined = round_both(project(spatial_norm, spatial_inproj))
    spatial_mixed = attend(spatial_joined.reshape(clip_count * FRAMES, PLACES, 3 * D))
    spatial_mixed = spatial_mixed.reshape(clip_count, FRAMES, PLACES, D)
    after_space = after_time + low_back(project(spatial_mixed, spatial_outproj) + spatial_biases[1])
    feed_norm = low(norm_rows(after_space, feed_gain, feed_biases[0]))
    hidden = low_back(project(feed_norm, widen_weight) + widen_bias)
    active = low(jax.nn.gelu(hidden, approximate=False))
    return after_space + low_back(project(active, narrow_weight) + feed_biases[1])

def reference(tokens, temporal_gain, temporal_biases, temporal_inproj, temporal_outproj, temporal_linear, spatial_gain, spatial_biases, spatial_inproj, spatial_outproj, feed_gain, feed_biases, widen_weight, widen_bias, narrow_weight, cotangent):
    parameters = tuple((item.astype(jnp.float32) for item in (temporal_gain, temporal_biases, temporal_inproj, temporal_outproj, temporal_linear, spatial_gain, spatial_biases, spatial_inproj, spatial_outproj, feed_gain, feed_biases, widen_weight, widen_bias, narrow_weight)))
    inputs = tokens.astype(jnp.float32)

    def forward(weights_all, inputs_all):
        groups = inputs_all.reshape(N_DP, CLIPS_DEV, FRAMES, PLACES, D)
        stepper = jax.checkpoint(lambda clip_block: layer(weights_all, clip_block))
        return lax.map(stepper, groups).reshape(inputs_all.shape)
    result, pullback = jax.vjp(forward, parameters, inputs)
    grads, grad_inputs = pullback(cotangent.astype(jnp.float32))
    return (result.astype(jnp.bfloat16), grad_inputs.astype(jnp.bfloat16), grads[0], grads[1], grads[2], grads[3], grads[4], grads[5], grads[6], grads[7], grads[8], grads[9], grads[10], grads[11], grads[12], grads[13])
```

```python
import functools

import jax
import jax.numpy as jnp
from jax import lax
from jax.sharding import PartitionSpec as P

HEADS = 12
HEAD_DIM = 64


def norm_rows(values, gain_row, bias_row):
    center = values - jnp.mean(values, axis=-1, keepdims=True)
    spread = jnp.mean(center * center, axis=-1, keepdims=True)
    return center * lax.rsqrt(spread + 1e-05) * gain_row + bias_row


def gelu_exact(values):
    return jax.nn.gelu(values, approximate=False)


def matmul(left_side, right_side):
    flattened = left_side.reshape(-1, left_side.shape[-1])
    result = jnp.dot(flattened, right_side, preferred_element_type=jnp.float32)
    return result.reshape(left_side.shape[:-1] + (right_side.shape[1],))


def times_transpose(left_side, right_side):
    flattened = left_side.reshape(-1, left_side.shape[-1])
    result = lax.dot_general(
        flattened, right_side, (((1,), (1,)), ((), ())), preferred_element_type=jnp.float32
    )
    return result.reshape(left_side.shape[:-1] + (right_side.shape[0],))


def outer_sum(left_side, right_side):
    return lax.dot_general(
        left_side.reshape(-1, left_side.shape[-1]),
        right_side.reshape(-1, right_side.shape[-1]),
        (((0,), (0,)), ((), ())),
        preferred_element_type=jnp.float32,
    )


def token_sum(values):
    return jnp.sum(values.astype(jnp.float32).reshape(-1, values.shape[-1]), axis=0)


def to_sequences(grid_array):
    clip_count, frame_count, place_count, width = grid_array.shape
    return jnp.transpose(grid_array, (0, 2, 1, 3)).reshape(
        clip_count * place_count, frame_count, width
    )


def to_grid(seq_array, clip_count):
    seq_count, frame_count, width = seq_array.shape
    return jnp.transpose(
        seq_array.reshape(clip_count, seq_count // clip_count, frame_count, width), (0, 2, 1, 3)
    )


def split_heads(joined):
    parted = joined.reshape(joined.shape[0], joined.shape[1], 3, HEADS, HEAD_DIM)
    return (parted[:, :, 0], parted[:, :, 1], parted[:, :, 2])


def score_rows(query_heads, key_heads):
    raw_scores = jnp.einsum(
        "blhd,bmhd->bhlm", query_heads, key_heads, preferred_element_type=jnp.float32
    )
    return raw_scores * HEAD_DIM ** (-0.5)


def attend_forward(joined):
    query_heads, key_heads, value_heads = split_heads(joined)
    scores = score_rows(query_heads, key_heads)
    row_max = jnp.max(scores, axis=-1, keepdims=True)
    log_total = jnp.log(jnp.sum(jnp.exp(scores - row_max), axis=-1, keepdims=True)) + row_max
    shares = jnp.exp(scores - log_total).astype(jnp.bfloat16)
    mixture = jnp.einsum("bhlm,bmhd->blhd", shares, value_heads, preferred_element_type=jnp.float32)
    return (
        mixture.reshape(joined.shape[0], joined.shape[1], HEADS * HEAD_DIM).astype(jnp.bfloat16),
        log_total,
    )


def attend_backward(joined, log_total, grad_mixture):
    query_heads, key_heads, value_heads = split_heads(joined)
    exact_shares = jnp.exp(score_rows(query_heads, key_heads) - log_total)
    shares = exact_shares.astype(jnp.bfloat16)
    grad_heads = grad_mixture.reshape(query_heads.shape)
    grad_values = jnp.einsum(
        "bhlm,blhd->bmhd", shares, grad_heads, preferred_element_type=jnp.float32
    )
    grad_shares = jnp.einsum(
        "blhd,bmhd->bhlm", grad_heads, value_heads, preferred_element_type=jnp.float32
    )
    row_terms = jnp.sum(grad_shares * exact_shares, axis=-1, keepdims=True)
    grad_scores = (exact_shares * (grad_shares - row_terms)).astype(jnp.bfloat16)
    scaling = HEAD_DIM ** (-0.5)
    grad_queries = (
        jnp.einsum("bhlm,bmhd->blhd", grad_scores, key_heads, preferred_element_type=jnp.float32)
        * scaling
    )
    grad_keys = (
        jnp.einsum("bhlm,blhd->bmhd", grad_scores, query_heads, preferred_element_type=jnp.float32)
        * scaling
    )
    stacked = jnp.stack([grad_queries, grad_keys, grad_values], axis=2)
    return stacked.reshape(joined.shape).astype(jnp.bfloat16)


def _vec_rows(vecs):
    return jnp.concatenate([v.reshape(-1, v.shape[-1]) for v in vecs], axis=0)


def on_device(n, tokens, tg, tb, t_in, t_out, t_lin, sg, sb, s_in, s_out, fg, fb, w1, b1, w2, cotangent):
    axes = ("dp", "seq")
    rows, width = t_in.shape[0], t_in.shape[0] * n
    parts = w2.shape[0] // rows
    hidden_units = w1.shape[1]

    def permute_cols(w):
        lead = w.shape[0]
        return w.reshape(lead, n, parts, rows).transpose(0, 2, 1, 3).reshape(lead, hidden_units)

    def unpermute_cols(w):
        lead = w.shape[0]
        return w.reshape(lead, parts, n, rows).transpose(0, 2, 1, 3).reshape(lead, hidden_units)

    w2_packed = w2.reshape(parts, rows, width).transpose(1, 0, 2).reshape(rows, parts * width)
    vecs = _vec_rows([tg[None], tb, sg[None], sb, fg[None], fb, b1.reshape(parts, rows)])
    n_vec = vecs.shape[0]
    vec_cols = jnp.pad(vecs.T, ((0, 0), (0, 128 - n_vec)))
    pack = jnp.concatenate([t_in, t_out, t_lin, s_in, s_out, permute_cols(w1), w2_packed, vec_cols], axis=1)
    full = lax.all_gather(pack, axes, axis=0, tiled=True)
    x = lax.all_to_all(tokens, "seq", split_axis=0, concat_axis=0, tiled=True)
    cot = lax.all_to_all(cotangent, "seq", split_axis=0, concat_axis=0, tiled=True)
    frames, places = x.shape[0] * x.shape[1], x.shape[2]
    x = x.reshape(1, frames, places, width)
    cot = cot.reshape(1, frames, places, width)
    c = [0]

    def take(k):
        c[0] += k
        return full[:, c[0] - k : c[0]]

    T_in, T_out, T_lin, S_in, S_out, W1 = take(3 * width), take(width), take(width), take(3 * width), take(width), take(hidden_units)
    W2 = jnp.concatenate([take(width) for _ in range(parts)], axis=0)
    V = take(128).astype(jnp.float32).T
    Tg, Tb, Sg, Sb, Fg, Fb = V[0], V[1:4], V[4], V[5:7], V[7], V[8:10]
    B1 = V[10 : 10 + parts].reshape(-1)
    bf = jnp.bfloat16

    inputs = x.astype(jnp.float32)
    norm_t = norm_rows(inputs, Tg, Tb[0]).astype(bf)
    joined_t = to_sequences(matmul(norm_t, T_in).astype(bf))
    mixed_t, lse_t = attend_forward(joined_t)
    mixed_g = to_grid(mixed_t, 1)
    proj_t = (matmul(mixed_g, T_out) + Tb[1]).astype(bf)
    branch_t = (matmul(proj_t, T_lin) + Tb[2]).astype(bf)
    after_time = inputs + branch_t.astype(jnp.float32)
    norm_s = norm_rows(after_time, Sg, Sb[0]).astype(bf)
    joined_s = matmul(norm_s, S_in).astype(bf).reshape(frames, places, -1)
    mixed_s, lse_s = attend_forward(joined_s)
    mixed_sg = mixed_s.reshape(after_time.shape)
    after_space = after_time + matmul(mixed_sg, S_out) + Sb[1]
    norm_m = norm_rows(after_space, Fg, Fb[0]).astype(bf)
    hidden = matmul(norm_m, W1) + B1
    active = gelu_exact(hidden).astype(bf)
    output = (after_space + matmul(active, W2) + Fb[1]).astype(bf)
    output = lax.all_to_all(output.reshape(tokens.shape), "seq", split_axis=0, concat_axis=0, tiled=True)

    def scatter(*grads):
        packed = jnp.concatenate([g.astype(bf) for g in grads], axis=1)
        return lax.psum_scatter(packed, axes, scatter_dimension=0, tiled=True).astype(jnp.float32)

    g_w2 = outer_sum(active, cot)
    g_fb1 = token_sum(cot)
    unused, gelu_pull = jax.vjp(gelu_exact, hidden)
    d_hidden = gelu_pull(times_transpose(cot, W2))[0].astype(bf)
    g_w1 = outer_sum(norm_m, d_hidden)
    g_b1 = token_sum(d_hidden)
    unused, pull = jax.vjp(norm_rows, after_space, Fg, Fb[0])
    d_norm, g_fg, g_fb0 = pull(times_transpose(d_hidden, W1))
    d_as = cot.astype(jnp.float32) + d_norm
    f_scat = scatter(g_w1, *[g_w2[j * width : (j + 1) * width] for j in range(parts)])

    d_space = d_as.astype(bf)
    g_sout = outer_sum(mixed_sg, d_space)
    g_sb1 = token_sum(d_space)
    d_mixed = times_transpose(d_space, S_out).astype(bf).reshape(mixed_s.shape)
    d_js = attend_backward(joined_s, lse_s, d_mixed)
    g_sin = outer_sum(norm_s, d_js)
    unused, pull = jax.vjp(norm_rows, after_time, Sg, Sb[0])
    d_norm, g_sg, g_sb0 = pull(times_transpose(d_js, S_in).reshape(after_time.shape))
    d_at = d_as + d_norm

    d_time = d_at.astype(bf)
    g_tlin = outer_sum(proj_t, d_time)
    g_tb2 = token_sum(d_time)
    d_proj = times_transpose(d_time, T_lin).astype(bf)
    g_tout = outer_sum(mixed_g, d_proj)
    g_tb1 = token_sum(d_proj)
    d_mt = to_sequences(times_transpose(d_proj, T_out).astype(bf))
    d_jt = to_grid(attend_backward(joined_t, lse_t, d_mt), 1)
    g_tin = outer_sum(norm_t, d_jt)
    d_nt = times_transpose(d_jt, T_in).astype(bf).astype(jnp.float32)
    unused, pull = jax.vjp(norm_rows, inputs, Tg, Tb[0])
    d_in, g_tg, g_tb0 = pull(d_nt)
    g_x = (d_at + d_in).astype(bf)
    g_x = lax.all_to_all(g_x.reshape(tokens.shape), "seq", split_axis=0, concat_axis=0, tiled=True)
    g_vec = jnp.concatenate(
        [jnp.stack([g_tg, g_tb0, g_tb1, g_tb2, g_sg, g_sb0, g_sb1, g_fg, g_fb0, g_fb1]), g_b1.reshape(parts, width)], axis=0
    )
    ts_scat = scatter(g_sin, g_sout, g_tin, g_tout, g_tlin, jnp.pad(g_vec.T, ((0, 0), (0, 128 - n_vec))))
    k = [0]

    def out(m):
        k[0] += m
        return ts_scat[:, k[0] - m : k[0]]

    o_sin, o_sout, o_tin, o_tout, o_tlin = out(3 * width), out(width), out(3 * width), out(width), out(width)
    v = out(128).T
    o_w1 = unpermute_cols(f_scat[:, :hidden_units])
    o_w2 = f_scat[:, hidden_units:].reshape(rows, parts, width).transpose(1, 0, 2).reshape(parts * rows, width)
    return (
        output, g_x, v[0], v[1:4], o_tin, o_tout, o_tlin, v[4], v[5:7], o_sin, o_sout, v[7], v[8:10],
        o_w1, v[10 : 10 + parts].reshape(-1), o_w2,
    )


def solution(mesh):
    shard = P(("dp", "seq"))
    cols = P(None, ("dp", "seq"))
    mat = P(("dp", "seq"), None)
    tok = P("dp", "seq", None, None)
    in_specs = (tok, shard, cols, mat, mat, mat, shard, cols, mat, mat, shard, cols, mat, shard, mat, tok)
    out_specs = (tok, tok, shard, cols, mat, mat, mat, shard, cols, mat, mat, shard, cols, mat, shard, mat)
    n = mesh.size
    return jax.shard_map(
        functools.partial(on_device, n), mesh=mesh, in_specs=in_specs, out_specs=out_specs, check_vma=False
    )
```

```python
import functools

import jax
import jax.numpy as jnp
from jax import lax
from jax.experimental import pallas as pl
from jax.experimental.pallas import tpu as pltpu
from jax.sharding import PartitionSpec as P

HEADS = 12
HEAD_DIM = 64
PAIR = 2 * HEAD_DIM
PAIRS = HEADS // 2
TILE = 16
GROUP_T = 6
GROUP_S = 2
GROUP_SB = 1
GROUP_TB = 3
LOW = -1e30
BF = jnp.bfloat16
F32 = jnp.float32


def dot_nn(a, b):
    return lax.dot_general(a, b, (((1,), (0,)), ((), ())), preferred_element_type=F32)


def dot_nt(a, b):
    return lax.dot_general(a, b, (((1,), (1,)), ((), ())), preferred_element_type=F32)


def dot_tn(a, b):
    return lax.dot_general(a, b, (((0,), (0,)), ((), ())), preferred_element_type=F32)


def normalize(values):
    center = values - jnp.mean(values, axis=-1, keepdims=True)
    scale = lax.rsqrt(jnp.mean(center * center, axis=-1, keepdims=True) + 1e-05)
    return center * scale, scale


def norm_back(unit, scale, gain, grad):
    graded = grad * gain
    shift = jnp.mean(graded, axis=-1, keepdims=True)
    slope = jnp.mean(graded * unit, axis=-1, keepdims=True)
    return scale * (graded - shift - unit * slope)


def rows_of(block):
    return block.reshape(block.shape[0] * block.shape[1], block.shape[2])


def col_sum(values):
    return jnp.sum(values, axis=0, keepdims=True)


def lane_halves(shape):
    return lax.broadcasted_iota(jnp.int32, shape, len(shape) - 1) < HEAD_DIM


def half_masks():
    low_half = lane_halves((1, PAIR))
    return (
        jnp.where(low_half, 1.0, 0.0).astype(BF),
        jnp.where(low_half, 0.0, 1.0).astype(BF),
    )


def heads_forward(tiles, bias):
    low_mask, high_mask = half_masks()
    scale = HEAD_DIM ** (-0.5)
    scores = []
    for query, key, value in tiles:
        for mask in (low_mask, high_mask):
            scores.append(dot_nt(query * (mask * scale), key) + bias)
    tops = [jnp.max(s, axis=-1, keepdims=True) for s in scores]
    shares = [jnp.exp(s - top).astype(BF) for s, top in zip(scores, tops)]
    outs = []
    for at, share in enumerate(shares):
        value = tiles[at // 2][2]
        outs.append(dot_nn(share, jnp.concatenate([value, jnp.ones_like(value)], axis=1)))
    mixed = []
    for at in range(len(tiles)):
        first, second = outs[2 * at], outs[2 * at + 1]
        low_half = lane_halves((first.shape[0], PAIR))
        top = jnp.where(low_half, first[:, :PAIR], second[:, :PAIR])
        total = jnp.where(low_half, first[:, PAIR:], second[:, PAIR:])
        mixed.append((top / total).astype(BF))
    return mixed


def heads_backward(tiles, bias):
    low_mask, high_mask = half_masks()
    scale = HEAD_DIM ** (-0.5)
    turned = [key.T for query, key, value, grad in tiles]
    queries, grads, scores, grad_shares = [], [], [], []
    for query, key, value, grad in tiles:
        for mask in (low_mask, high_mask):
            queries.append(query * (mask * scale))
            grads.append(grad * mask)
            scores.append(dot_nt(key, queries[-1]) + bias)
            grad_shares.append(dot_nt(value, grads[-1]))
    tops = [jnp.max(s, axis=0, keepdims=True) for s in scores]
    raw = [jnp.exp(s - top) for s, top in zip(scores, tops)]
    inverse = [1.0 / jnp.sum(e, axis=0, keepdims=True) for e in raw]
    shares = [e * i for e, i in zip(raw, inverse)]
    terms = [jnp.sum(g * p, axis=0, keepdims=True) for g, p in zip(grad_shares, shares)]
    grad_scores = [(p * (g - t)).astype(BF) for p, g, t in zip(shares, grad_shares, terms)]
    shares = [p.astype(BF) for p in shares]
    out = []
    for at in range(len(tiles)):
        a, b = 2 * at, 2 * at + 1
        grad_value = dot_nn(shares[a], grads[a]) + dot_nn(shares[b], grads[b])
        grad_key = dot_nn(grad_scores[a], queries[a]) + dot_nn(grad_scores[b], queries[b])
        key_turned = turned[at]
        grad_query = jnp.concatenate(
            [dot_nn(key_turned[:HEAD_DIM], grad_scores[a]), dot_nn(key_turned[HEAD_DIM:], grad_scores[b])], axis=0
        )
        out.append(((grad_query * scale).astype(BF).T, grad_key.astype(BF), grad_value.astype(BF)))
    return out


def place_mask(size):
    row = lax.broadcasted_iota(jnp.int32, (size, size), 0)
    col = lax.broadcasted_iota(jnp.int32, (size, size), 1)
    return jnp.where(((row ^ col) & (TILE - 1)) == 0, 0.0, LOW)


def pair_cols(part, pair, width):
    start = part * width + pair * PAIR
    return slice(start, start + PAIR)


def temporal_forward(chunk, x_ref, qk_ref, v_in_ref, ol_ref, v_ref, norm_ref, joined_ref, mixed_ref, proj_ref, after_ref):
    frames, padded, width = x_ref.shape
    steps = frames // chunk

    def project(c, carry):
        at = pl.ds(c * chunk, chunk)
        unit, scale = normalize(rows_of(x_ref[at]).astype(F32))
        norm = (unit * v_ref[0:1] + v_ref[1:2]).astype(BF)
        norm_ref[at] = norm.reshape(chunk, padded, width)
        for part in range(3):
            cols = slice(part * width, (part + 1) * width)
            weight = qk_ref[:, cols] if part < 2 else v_in_ref[:, :width]
            joined_ref[at, :, cols] = dot_nn(norm, weight).astype(BF).reshape(chunk, padded, width)
        return carry

    lax.fori_loop(0, steps, project, 0)

    def attend(g, carry):
        at = pl.ds(pl.multiple_of(g * TILE, TILE), TILE)
        allowed = place_mask(frames * TILE)
        for first in range(0, PAIRS, GROUP_T):
            group = range(first, first + GROUP_T)
            tiles = [[rows_of(joined_ref[:, at, pair_cols(i, pair, width)]) for i in range(3)] for pair in group]
            for pair, mixed in zip(group, heads_forward(tiles, allowed)):
                mixed_ref[:, at, pair_cols(0, pair, width)] = mixed.reshape(frames, TILE, PAIR)
        return carry

    lax.fori_loop(0, padded // TILE, attend, 0)

    def finish(c, carry):
        at = pl.ds(c * chunk, chunk)
        mixed = rows_of(mixed_ref[at])
        proj = (dot_nn(mixed, ol_ref[:, :width]) + v_ref[2:3]).astype(BF)
        proj_ref[at] = proj.reshape(chunk, padded, width)
        branch = (dot_nn(proj, ol_ref[:, width:]) + v_ref[3:4]).astype(BF)
        after = rows_of(x_ref[at]).astype(F32) + branch.astype(F32)
        after_ref[at] = after.reshape(chunk, padded, width)
        return carry

    lax.fori_loop(0, steps, finish, 0)


def spatial_forward(places, after_ref, qk_ref, vo_ref, v_ref, norm_ref, joined_ref, mixed_ref, space_ref):
    chunk, padded, width = after_ref.shape
    after = rows_of(after_ref[...])
    unit, scale = normalize(after)
    norm = (unit * v_ref[4:5] + v_ref[5:6]).astype(BF)
    norm_ref[...] = norm.reshape(chunk, padded, width)
    for part in range(3):
        cols = slice(part * width, (part + 1) * width)
        weight = qk_ref[:, cols] if part < 2 else vo_ref[:, :width]
        joined_ref[:, :, cols] = dot_nn(norm, weight).astype(BF).reshape(chunk, padded, width)
    allowed = jnp.where(lax.broadcasted_iota(jnp.int32, (1, padded), 1) < places, 0.0, LOW)
    for frame in range(chunk):
        for first in range(0, PAIRS, GROUP_S):
            group = range(first, first + GROUP_S)
            tiles = [[joined_ref[frame, :, pair_cols(i, pair, width)] for i in range(3)] for pair in group]
            for pair, mixed in zip(group, heads_forward(tiles, allowed)):
                mixed_ref[frame, :, pair_cols(0, pair, width)] = mixed
    space = after + dot_nn(rows_of(mixed_ref[...]), vo_ref[:, width:]) + v_ref[6:7]
    space_ref[...] = space.reshape(chunk, padded, width)


def gelu_parts(hidden):
    phi = 0.5 * (1.0 + lax.erf(hidden * 0.7071067811865476))
    density = jnp.exp(-0.5 * hidden * hidden) * 0.3989422804014327
    return phi, density


def feed_both(places, space_ref, cot_ref, w1_ref, w2_ref, v_ref, out_ref, grad_ref, norm_ref, active_ref, dhid_ref, vec_ref):
    chunk, padded, width = space_ref.shape
    blocks = w1_ref.shape[1] // width

    @pl.when(pl.program_id(0) == 0)
    def _():
        vec_ref[...] = jnp.zeros_like(vec_ref)

    space = rows_of(space_ref[...])
    cot = rows_of(cot_ref[...])
    unit, scale = normalize(space)
    norm = (unit * v_ref[7:8] + v_ref[8:9]).astype(BF)
    norm_ref[...] = norm.reshape(chunk, padded, width)
    out = space + v_ref[9:10]
    d_norm = jnp.zeros_like(space)
    for block in range(blocks):
        cols = slice(block * width, (block + 1) * width)
        hidden = dot_nn(norm, w1_ref[:, cols]) + v_ref[10 + block : 11 + block]
        phi, density = gelu_parts(hidden)
        active = (hidden * phi).astype(BF)
        active_ref[:, :, cols] = active.reshape(chunk, padded, width)
        out += dot_nn(active, w2_ref[:, cols])
        d_hidden = dot_nt(cot, w2_ref[:, cols]) * (phi + hidden * density)
        vec_ref[3 + block : 4 + block] += col_sum(d_hidden.astype(BF).astype(F32))
        d_hidden = d_hidden.astype(BF)
        dhid_ref[:, :, cols] = d_hidden.reshape(chunk, padded, width)
        d_norm += dot_nt(d_hidden, w1_ref[:, cols])
    for frame in range(chunk):
        out_ref[frame] = out[frame * padded : frame * padded + places].astype(BF)
    vec_ref[0:1] += col_sum(d_norm * unit)
    vec_ref[1:2] += col_sum(d_norm)
    vec_ref[2:3] += col_sum(cot.astype(F32))
    grad = cot.astype(F32) + norm_back(unit, scale, v_ref[7:8], d_norm)
    grad_ref[...] = grad.reshape(chunk, padded, width)


def feed_grads(norm_ref, dhid_ref, active_ref, cot_ref, out_ref, norm_turned, cot_turned):
    width = norm_ref.shape[1]

    @pl.when(pl.program_id(0) == 0)
    def _():
        norm_turned[...] = norm_ref[...].T
        cot_turned[...] = cot_ref[...].T

    out_ref[:, :width] = dot_nn(norm_turned[...], dhid_ref[...]).astype(BF)
    out_ref[:, width:] = dot_nn(cot_turned[...], active_ref[...]).astype(BF).T


def spatial_back(places, grad_ref, after_ref, joined_ref, qk_ref, vo_ref, v_ref, dspace_ref, djoin_ref, dat_ref, dtime_ref, vec_ref, dmix_ref):
    chunk, padded, width = grad_ref.shape

    @pl.when(pl.program_id(0) == 0)
    def _():
        vec_ref[...] = jnp.zeros_like(vec_ref)

    grad = rows_of(grad_ref[...])
    d_space = grad.astype(BF)
    dspace_ref[...] = d_space.reshape(chunk, padded, width)
    vec_ref[2:3] += col_sum(d_space.astype(F32))
    dmix_ref[...] = dot_nt(d_space, vo_ref[:, width:]).astype(BF).reshape(chunk, padded, width)
    allowed = jnp.where(lax.broadcasted_iota(jnp.int32, (padded, 1), 0) < places, 0.0, LOW)
    for frame in range(chunk):
        for first in range(0, PAIRS, GROUP_SB):
            group = range(first, first + GROUP_SB)
            tiles = [
                [joined_ref[frame, :, pair_cols(i, pair, width)] for i in range(3)]
                + [dmix_ref[frame, :, pair_cols(0, pair, width)]]
                for pair in group
            ]
            for pair, grads in zip(group, heads_backward(tiles, allowed)):
                for i in range(3):
                    djoin_ref[frame, :, pair_cols(i, pair, width)] = grads[i]
    d_joined = rows_of(djoin_ref[...])
    d_norm = dot_nt(d_joined[:, : 2 * width], qk_ref[...]) + dot_nt(d_joined[:, 2 * width :], vo_ref[:, :width])
    unit, scale = normalize(rows_of(after_ref[...]))
    vec_ref[0:1] += col_sum(d_norm * unit)
    vec_ref[1:2] += col_sum(d_norm)
    d_time = grad + norm_back(unit, scale, v_ref[4:5], d_norm)
    dat_ref[...] = d_time.reshape(chunk, padded, width)
    dtime_ref[...] = d_time.astype(BF).reshape(chunk, padded, width)


def join_grads(norm_ref, djoin_ref, mixed_ref, dspace_ref, out_ref, norm_turned):
    i = pl.program_id(0)
    parts = 3

    @pl.when(i == 0)
    def _():
        norm_turned[...] = norm_ref[...].T

    @pl.when(i < parts)
    def _():
        out_ref[...] = dot_nn(norm_turned[...], djoin_ref[...]).astype(BF)

    @pl.when(i == parts)
    def _():
        out_ref[...] = dot_tn(mixed_ref[...], dspace_ref[...]).astype(BF)


def temporal_back(chunk, places, dat_ref, dtime_ref, x_ref, joined_ref, qk_ref, v_in_ref, ol_ref, v_ref, dproj_ref, djoin_ref, gx_ref, vec_ref, dmix_ref):
    frames, padded, width = x_ref.shape
    steps = frames // chunk
    vec_ref[...] = jnp.zeros_like(vec_ref)

    def project(c, carry):
        at = pl.ds(c * chunk, chunk)
        d_time = rows_of(dtime_ref[at])
        vec_ref[3:4] += col_sum(d_time.astype(F32))
        d_proj = dot_nt(d_time, ol_ref[:, width:]).astype(BF)
        vec_ref[2:3] += col_sum(d_proj.astype(F32))
        dproj_ref[at] = d_proj.reshape(chunk, padded, width)
        d_mixed = dot_nt(d_proj, ol_ref[:, :width]).astype(BF)
        dmix_ref[at] = d_mixed.reshape(chunk, padded, width)
        return carry

    lax.fori_loop(0, steps, project, 0)

    def attend(g, carry):
        at = pl.ds(pl.multiple_of(g * TILE, TILE), TILE)
        allowed = place_mask(frames * TILE)
        for first in range(0, PAIRS, GROUP_TB):
            group = range(first, first + GROUP_TB)
            tiles = [
                [rows_of(joined_ref[:, at, pair_cols(i, pair, width)]) for i in range(3)]
                + [rows_of(dmix_ref[:, at, pair_cols(0, pair, width)])]
                for pair in group
            ]
            for pair, grads in zip(group, heads_backward(tiles, allowed)):
                for i in range(3):
                    djoin_ref[:, at, pair_cols(i, pair, width)] = grads[i].reshape(frames, TILE, PAIR)
        return carry

    lax.fori_loop(0, padded // TILE, attend, 0)

    def finish(c, carry):
        at = pl.ds(c * chunk, chunk)
        d_joined = rows_of(djoin_ref[at])
        d_norm = dot_nt(d_joined[:, : 2 * width], qk_ref[...]) + dot_nt(d_joined[:, 2 * width :], v_in_ref[:, :width])
        d_norm = d_norm.astype(BF).astype(F32)
        unit, scale = normalize(rows_of(x_ref[at]).astype(F32))
        vec_ref[0:1] += col_sum(d_norm * unit)
        vec_ref[1:2] += col_sum(d_norm)
        grad = rows_of(dat_ref[at]) + norm_back(unit, scale, v_ref[0:1], d_norm)
        grad = grad.astype(BF).reshape(chunk, padded, width)
        gx_ref[at] = grad[:, :places]
        return carry

    lax.fori_loop(0, steps, finish, 0)


def whole(shape):
    return pl.BlockSpec(shape, lambda *i: (0,) * len(shape))


def params(mib=60):
    return pltpu.CompilerParams(vmem_limit_bytes=mib << 20)


def shape_of(*dims, dtype=BF):
    return jax.ShapeDtypeStruct(dims, dtype)


def run_temporal_forward(x, weights, v, chunk=2):
    frames, padded, width = x.shape
    dims = (frames, padded, width)
    wide = (frames, padded, 3 * width)
    return pl.pallas_call(
        functools.partial(temporal_forward, chunk),
        out_shape=(shape_of(*dims), shape_of(*wide), shape_of(*dims), shape_of(*dims), shape_of(*dims, dtype=F32)),
        compiler_params=params(),
    )(x, *weights, v)


def frame_block(chunk, padded, width):
    return pl.BlockSpec((chunk, padded, width), lambda i: (i, 0, 0))


def run_spatial_forward(places, after, weights, v, chunk=2):
    frames, padded, width = after.shape
    block = frame_block(chunk, padded, width)
    wide = frame_block(chunk, padded, 3 * width)
    dims = (frames, padded, width)
    return pl.pallas_call(
        functools.partial(spatial_forward, places),
        grid=(frames // chunk,),
        in_specs=[block] + [whole(w.shape) for w in weights] + [whole(v.shape)],
        out_specs=[block, wide, block, block],
        out_shape=(shape_of(*dims), shape_of(frames, padded, 3 * width), shape_of(*dims), shape_of(*dims, dtype=F32)),
        compiler_params=params(),
    )(after, *weights, v)


def run_feed(places, space, cot, pack, v, chunk=2):
    frames, padded, width = space.shape
    hidden = 4 * width
    block = frame_block(chunk, padded, width)
    wide = frame_block(chunk, padded, hidden)
    dims = (frames, padded, width)
    return pl.pallas_call(
        functools.partial(feed_both, places),
        grid=(frames // chunk,),
        in_specs=[
            block, block,
            pl.BlockSpec((width, hidden), lambda i: (0, 0)),
            pl.BlockSpec((width, hidden), lambda i: (0, 1)),
            whole(v.shape),
        ],
        out_specs=[frame_block(chunk, places, width), block, block, wide, wide, whole((8, width))],
        out_shape=(
            shape_of(frames, places, width), shape_of(*dims, dtype=F32), shape_of(*dims),
            shape_of(frames, padded, hidden), shape_of(frames, padded, hidden), shape_of(8, width, dtype=F32),
        ),
        compiler_params=params(),
    )(space, cot, pack, pack, v)


def flat(a):
    return a.reshape(-1, a.shape[-1])


def run_feed_grads(norm, d_hidden, active, cot):
    norm, d_hidden, active, cot = flat(norm), flat(d_hidden), flat(active), flat(cot)
    rows, width = norm.shape
    blocks = d_hidden.shape[1] // width
    part = pl.BlockSpec((rows, width), lambda i: (0, i))
    return pl.pallas_call(
        feed_grads,
        grid=(blocks,),
        in_specs=[whole((rows, width)), part, part, whole((rows, width))],
        out_specs=pl.BlockSpec((width, 2 * width), lambda i: (0, i)),
        out_shape=shape_of(width, 2 * width * blocks),
        scratch_shapes=[pltpu.VMEM((width, rows), BF), pltpu.VMEM((width, rows), BF)],
        compiler_params=params(),
    )(norm, d_hidden, active, cot)


def run_spatial_back(places, grad, after, joined, weights, v, chunk=2):
    frames, padded, width = grad.shape
    block = frame_block(chunk, padded, width)
    wide = frame_block(chunk, padded, 3 * width)
    dims = (frames, padded, width)
    return pl.pallas_call(
        functools.partial(spatial_back, places),
        grid=(frames // chunk,),
        in_specs=[block, block, wide] + [whole(w.shape) for w in weights] + [whole(v.shape)],
        out_specs=[block, wide, block, block, whole((8, width))],
        out_shape=(
            shape_of(*dims), shape_of(frames, padded, 3 * width), shape_of(*dims, dtype=F32), shape_of(*dims),
            shape_of(8, width, dtype=F32),
        ),
        scratch_shapes=[pltpu.VMEM((chunk, padded, width), BF)],
        compiler_params=params(),
    )(grad, after, joined, *weights, v)


def run_join_grads(norm, d_joined, mixed, d_out):
    norm, d_joined, mixed, d_out = flat(norm), flat(d_joined), flat(mixed), flat(d_out)
    rows, width = norm.shape
    return pl.pallas_call(
        join_grads,
        grid=(4,),
        in_specs=[
            whole((rows, width)), pl.BlockSpec((rows, width), lambda i: (0, jnp.minimum(i, 2))),
            whole((rows, width)), whole((rows, width)),
        ],
        out_specs=pl.BlockSpec((width, width), lambda i: (0, i)),
        out_shape=shape_of(width, 4 * width),
        scratch_shapes=[pltpu.VMEM((width, rows), BF)],
        compiler_params=params(),
    )(norm, d_joined, mixed, d_out)


def run_temporal_back(places, d_at, d_time, x, joined, weights, v, chunk=2):
    frames, padded, width = x.shape
    dims = (frames, padded, width)
    return pl.pallas_call(
        functools.partial(temporal_back, chunk, places),
        out_shape=(
            shape_of(*dims), shape_of(frames, padded, 3 * width), shape_of(frames, places, width),
            shape_of(8, width, dtype=F32),
        ),
        scratch_shapes=[pltpu.VMEM(dims, BF)],
        compiler_params=params(),
    )(d_at, d_time, x, joined, *weights, v)


def tile_grad(a_ref, b_ref, out_ref):
    out_ref[...] = dot_tn(a_ref[...], b_ref[...]).astype(BF)


def run_tile_grad(a, b):
    a, b = flat(a), flat(b)
    rows, width = a.shape
    return pl.pallas_call(
        tile_grad,
        grid=(2,),
        in_specs=[pl.BlockSpec((rows, width // 2), lambda i: (0, i)), whole((rows, b.shape[1]))],
        out_specs=pl.BlockSpec((width // 2, b.shape[1]), lambda i: (i, 0)),
        out_shape=shape_of(width, b.shape[1]),
        compiler_params=params(),
    )(a, b)


AXES = ("dp", "seq")


def swap(values, bit, n):
    return lax.ppermute(values, AXES, [(i, i ^ (1 << bit)) for i in range(n)])


def gather_rows(values, n, order):
    bits = n.bit_length() - 1
    me = lax.axis_index(AXES)
    held = values.reshape((1,) * bits + values.shape)
    for bit in order:
        axis = bits - 1 - bit
        other = swap(held, bit, n)
        high = ((me >> bit) & 1) == 1
        held = jnp.where(high, jnp.concatenate([other, held], axis), jnp.concatenate([held, other], axis))
    return held.reshape((n * values.shape[0],) + values.shape[1:])


def scatter_rows(values, n, order):
    bits = n.bit_length() - 1
    me = lax.axis_index(AXES)
    rows = values.shape[0] // n
    held = values.reshape((2,) * bits + (rows,) + values.shape[1:])
    for bit in order:
        axis = bits - 1 - bit
        mine = (me >> bit) & 1
        send = lax.dynamic_index_in_dim(held, 1 - mine, axis, keepdims=True)
        keep = lax.dynamic_index_in_dim(held, mine, axis, keepdims=True)
        held = (keep.astype(F32) + swap(send, bit, n).astype(F32)).astype(values.dtype)
    return held.reshape((rows,) + values.shape[1:])


def on_device(n, tokens, tg, tb, t_in, t_out, t_lin, sg, sb, s_in, s_out, fg, fb, w1, b1, w2, cotangent):
    bits = n.bit_length() - 1
    top = tuple(range(bits - 1, 2, -1))
    order_a, order_b, order_c = top + (1, 2, 0), top + (2, 1, 0), (1, 2) + top + (0,)
    rows, width = t_in.shape[0], t_in.shape[0] * n
    parts = w2.shape[0] // rows
    hidden = w1.shape[1]
    places = tokens.shape[2]
    frames = tokens.shape[0] * tokens.shape[1]
    extra = -places % TILE

    vecs = jnp.concatenate([tg[None], tb, sg[None], sb, fg[None], fb, b1.reshape(parts, rows)], axis=0)
    n_vec = vecs.shape[0]
    vec_cols = jnp.pad(vecs.T, ((0, 0), (0, 2 * HEAD_DIM - n_vec)))
    feed = jnp.concatenate(
        [
            w1.reshape(rows, n, parts, rows).transpose(0, 2, 1, 3).reshape(rows, hidden),
            w2.reshape(parts, rows, width).transpose(1, 0, 2).reshape(rows, hidden),
        ],
        axis=1,
    )
    feed = lax.all_gather(feed, AXES, axis=0, tiled=True)

    def own_clip(grid):
        clip = lax.all_to_all(grid, "seq", split_axis=0, concat_axis=0, tiled=True)
        return jnp.pad(clip.reshape(frames, places, width), ((0, 0), (0, extra), (0, 0)))

    def own_frames(clip):
        return lax.all_to_all(clip.reshape(tokens.shape), "seq", split_axis=0, concat_axis=0, tiled=True)

    x = own_clip(tokens)
    t_w = (
        gather_rows(t_in[:, : 2 * width], n, order_a),
        gather_rows(jnp.concatenate([t_in[:, 2 * width :], vec_cols], axis=1), n, order_c),
        gather_rows(jnp.concatenate([t_out, t_lin], axis=1), n, order_b),
    )
    s_w = (
        gather_rows(s_in[:, : 2 * width], n, order_a),
        gather_rows(jnp.concatenate([s_in[:, 2 * width :], s_out], axis=1), n, order_b),
    )
    cot = own_clip(cotangent)
    vec = t_w[1][:, width:].T[:16].astype(F32)

    norm_t, joined_t, mixed_t, proj_t, after_time = run_temporal_forward(x, t_w, vec)
    norm_s, joined_s, mixed_s, after_space = run_spatial_forward(places, after_time, s_w, vec)
    out, d_after_space, norm_m, active, d_hidden, vec_f = run_feed(places, after_space, cot, feed, vec)
    output = own_frames(out)
    g_feed = run_feed_grads(norm_m, d_hidden, active, cot)
    g_feed = lax.psum_scatter(g_feed, AXES, scatter_dimension=0, tiled=True).astype(F32)
    d_space, d_joined_s, d_after_time, d_time, vec_s = run_spatial_back(
        places, d_after_space, after_time, joined_s, s_w, vec
    )
    g_lin = run_tile_grad(proj_t, d_time)
    g_space = run_join_grads(norm_s, d_joined_s, mixed_s, d_space)
    g_space = jnp.concatenate(
        [
            scatter_rows(g_space[:, : 2 * width], n, order_a[::-1]),
            scatter_rows(g_space[:, 2 * width :], n, order_b[::-1]),
        ],
        axis=1,
    ).astype(F32)
    d_proj, d_joined_t, g_x, vec_t = run_temporal_back(places, d_after_time, d_time, x, joined_t, t_w, vec)
    g_x = own_frames(g_x)
    g_time = run_join_grads(norm_t, d_joined_t, mixed_t, d_proj)
    g_vec = jnp.concatenate([vec_t[:4], vec_s[:3], vec_f[: 3 + parts]], axis=0)
    g_vec = jnp.pad(g_vec.T.astype(BF), ((0, 0), (0, 2 * HEAD_DIM - n_vec)))
    g_last = scatter_rows(jnp.concatenate([g_lin, g_vec], axis=1), n, order_c[::-1]).astype(F32)
    g_time = jnp.concatenate(
        [
            scatter_rows(g_time[:, : 2 * width], n, order_a[::-1]),
            scatter_rows(g_time[:, 2 * width :], n, order_b[::-1]),
        ],
        axis=1,
    ).astype(F32)
    v = g_last[:, width : width + n_vec].T
    g_feed = g_feed.reshape(rows, parts, 2, width)
    o_w1 = g_feed[:, :, 0].reshape(rows, parts, n, rows).transpose(0, 2, 1, 3).reshape(rows, hidden)
    o_w2 = g_feed[:, :, 1].transpose(1, 0, 2).reshape(parts * rows, width)
    return (
        output, g_x, v[0], v[1:4], g_time[:, : 3 * width], g_time[:, 3 * width :], g_last[:, :width],
        v[4], v[5:7], g_space[:, : 3 * width], g_space[:, 3 * width :], v[7], v[8:10],
        o_w1, v[10 : 10 + parts].reshape(-1), o_w2,
    )


def solution(mesh):
    shard = P(("dp", "seq"))
    cols = P(None, ("dp", "seq"))
    mat = P(("dp", "seq"), None)
    tok = P("dp", "seq", None, None)
    in_specs = (tok, shard, cols, mat, mat, mat, shard, cols, mat, mat, shard, cols, mat, shard, mat, tok)
    out_specs = (tok, tok, shard, cols, mat, mat, mat, shard, cols, mat, mat, shard, cols, mat, shard, mat)
    return jax.shard_map(
        functools.partial(on_device, mesh.size), mesh=mesh, in_specs=in_specs, out_specs=out_specs, check_vma=False
    )
```

```python
import functools

import jax
import jax.numpy as jnp
from jax import lax
from jax.experimental import pallas as pl
from jax.experimental.pallas import tpu as pltpu
from jax.sharding import PartitionSpec as P

HEADS = 12
HEAD_DIM = 64
PAIR = 2 * HEAD_DIM
PAIRS = HEADS // 2
TILE = 16
GROUP_T = 6
GROUP_S = 2
GROUP_SB = 1
GROUP_TB = 3
LOW = -1e30
BF = jnp.bfloat16
F32 = jnp.float32


def dot_nn(a, b):
    return lax.dot_general(a, b, (((1,), (0,)), ((), ())), preferred_element_type=F32)


def dot_nt(a, b):
    return lax.dot_general(a, b, (((1,), (1,)), ((), ())), preferred_element_type=F32)


def dot_tn(a, b):
    return lax.dot_general(a, b, (((0,), (0,)), ((), ())), preferred_element_type=F32)


def normalize(values):
    center = values - jnp.mean(values, axis=-1, keepdims=True)
    scale = lax.rsqrt(jnp.mean(center * center, axis=-1, keepdims=True) + 1e-05)
    return center * scale, scale


def norm_back(unit, scale, gain, grad):
    graded = grad * gain
    shift = jnp.mean(graded, axis=-1, keepdims=True)
    slope = jnp.mean(graded * unit, axis=-1, keepdims=True)
    return scale * (graded - shift - unit * slope)


def rows_of(block):
    return block.reshape(block.shape[0] * block.shape[1], block.shape[2])


def col_sum(values):
    return jnp.sum(values, axis=0, keepdims=True)


def lane_halves(shape):
    return lax.broadcasted_iota(jnp.int32, shape, len(shape) - 1) < HEAD_DIM


def half_masks():
    low_half = lane_halves((1, PAIR))
    return (
        jnp.where(low_half, 1.0, 0.0).astype(BF),
        jnp.where(low_half, 0.0, 1.0).astype(BF),
    )


def heads_forward(tiles, bias):
    low_mask, high_mask = half_masks()
    scale = HEAD_DIM ** (-0.5)
    scores = []
    for query, key, value in tiles:
        for mask in (low_mask, high_mask):
            scores.append(dot_nt(query * (mask * scale), key) + bias)
    tops = [jnp.max(s, axis=-1, keepdims=True) for s in scores]
    shares = [jnp.exp(s - top).astype(BF) for s, top in zip(scores, tops)]
    outs = []
    for at, share in enumerate(shares):
        value = tiles[at // 2][2]
        outs.append(dot_nn(share, jnp.concatenate([value, jnp.ones_like(value)], axis=1)))
    mixed = []
    for at in range(len(tiles)):
        first, second = outs[2 * at], outs[2 * at + 1]
        low_half = lane_halves((first.shape[0], PAIR))
        top = jnp.where(low_half, first[:, :PAIR], second[:, :PAIR])
        total = jnp.where(low_half, first[:, PAIR:], second[:, PAIR:])
        mixed.append((top / total).astype(BF))
    return mixed


def heads_backward(tiles, bias):
    low_mask, high_mask = half_masks()
    scale = HEAD_DIM ** (-0.5)
    turned = [key.T for query, key, value, grad in tiles]
    queries, grads, scores, grad_shares = [], [], [], []
    for query, key, value, grad in tiles:
        for mask in (low_mask, high_mask):
            queries.append(query * (mask * scale))
            grads.append(grad * mask)
            scores.append(dot_nt(key, queries[-1]) + bias)
            grad_shares.append(dot_nt(value, grads[-1]))
    tops = [jnp.max(s, axis=0, keepdims=True) for s in scores]
    raw = [jnp.exp(s - top) for s, top in zip(scores, tops)]
    inverse = [1.0 / jnp.sum(e, axis=0, keepdims=True) for e in raw]
    shares = [e * i for e, i in zip(raw, inverse)]
    terms = [jnp.sum(g * p, axis=0, keepdims=True) for g, p in zip(grad_shares, shares)]
    grad_scores = [(p * (g - t)).astype(BF) for p, g, t in zip(shares, grad_shares, terms)]
    shares = [p.astype(BF) for p in shares]
    out = []
    for at in range(len(tiles)):
        a, b = 2 * at, 2 * at + 1
        grad_value = dot_nn(shares[a], grads[a]) + dot_nn(shares[b], grads[b])
        grad_key = dot_nn(grad_scores[a], queries[a]) + dot_nn(grad_scores[b], queries[b])
        key_turned = turned[at]
        grad_query = jnp.concatenate(
            [dot_nn(key_turned[:HEAD_DIM], grad_scores[a]), dot_nn(key_turned[HEAD_DIM:], grad_scores[b])], axis=0
        )
        out.append(((grad_query * scale).astype(BF).T, grad_key.astype(BF), grad_value.astype(BF)))
    return out


def place_mask(size):
    row = lax.broadcasted_iota(jnp.int32, (size, size), 0)
    col = lax.broadcasted_iota(jnp.int32, (size, size), 1)
    return jnp.where(((row ^ col) & (TILE - 1)) == 0, 0.0, LOW)


def pair_cols(part, pair, width):
    start = part * width + pair * PAIR
    return slice(start, start + PAIR)


def temporal_project(x_ref, qk_ref, v_in_ref, v_ref, norm_ref, joined_ref):
    chunk, padded, width = x_ref.shape
    unit, scale = normalize(rows_of(x_ref[...]).astype(F32))
    norm = (unit * v_ref[0:1] + v_ref[1:2]).astype(BF)
    norm_ref[...] = norm.reshape(chunk, padded, width)
    for part in range(3):
        cols = slice(part * width, (part + 1) * width)
        weight = qk_ref[:, cols] if part < 2 else v_in_ref[:, :width]
        joined_ref[:, :, cols] = dot_nn(norm, weight).astype(BF).reshape(chunk, padded, width)


def temporal_attend(joined_ref, mixed_ref):
    frames, tile, width = mixed_ref.shape
    bias = place_mask(frames * tile)
    for first in range(0, PAIRS, GROUP_T):
        group = range(first, first + GROUP_T)
        tiles = [[rows_of(joined_ref[:, :, pair_cols(i, pair, width)]) for i in range(3)] for pair in group]
        for pair, mixed in zip(group, heads_forward(tiles, bias)):
            mixed_ref[:, :, pair_cols(0, pair, width)] = mixed.reshape(frames, tile, PAIR)


def temporal_finish(x_ref, mixed_ref, ol_ref, v_ref, proj_ref, after_ref):
    chunk, padded, width = x_ref.shape
    proj = (dot_nn(rows_of(mixed_ref[...]), ol_ref[:, :width]) + v_ref[2:3]).astype(BF)
    proj_ref[...] = proj.reshape(chunk, padded, width)
    branch = (dot_nn(proj, ol_ref[:, width:]) + v_ref[3:4]).astype(BF)
    after = rows_of(x_ref[...]).astype(F32) + branch.astype(F32)
    after_ref[...] = after.reshape(chunk, padded, width)


def spatial_forward(places, after_ref, s_ref, v_ref, norm_ref, joined_ref, mixed_ref, space_ref):
    chunk, padded, width = after_ref.shape
    after = rows_of(after_ref[...])
    unit, scale = normalize(after)
    norm = (unit * v_ref[4:5] + v_ref[5:6]).astype(BF)
    norm_ref[...] = norm.reshape(chunk, padded, width)
    for part in range(3):
        cols = slice(part * width, (part + 1) * width)
        joined_ref[:, :, cols] = dot_nn(norm, s_ref[:, cols]).astype(BF).reshape(chunk, padded, width)
    allowed = jnp.where(lax.broadcasted_iota(jnp.int32, (1, padded), 1) < places, 0.0, LOW)
    for frame in range(chunk):
        for first in range(0, PAIRS, GROUP_S):
            group = range(first, first + GROUP_S)
            tiles = [[joined_ref[frame, :, pair_cols(i, pair, width)] for i in range(3)] for pair in group]
            for pair, mixed in zip(group, heads_forward(tiles, allowed)):
                mixed_ref[frame, :, pair_cols(0, pair, width)] = mixed
    space = after + dot_nn(rows_of(mixed_ref[...]), s_ref[:, 3 * width :]) + v_ref[6:7]
    space_ref[...] = space.reshape(chunk, padded, width)


def gelu_parts(hidden):
    phi = 0.5 * (1.0 + lax.erf(hidden * 0.7071067811865476))
    density = jnp.exp(-0.5 * hidden * hidden) * 0.3989422804014327
    return phi, density


def feed_both(places, space_ref, cot_ref, w1_ref, w2_ref, v_ref, out_ref, grad_ref, norm_ref, active_ref, dhid_ref, vec_ref):
    chunk, padded, width = space_ref.shape
    blocks = w1_ref.shape[1] // width

    @pl.when(pl.program_id(0) == 0)
    def _():
        vec_ref[...] = jnp.zeros_like(vec_ref)

    space = rows_of(space_ref[...])
    cot = rows_of(cot_ref[...])
    unit, scale = normalize(space)
    norm = (unit * v_ref[7:8] + v_ref[8:9]).astype(BF)
    norm_ref[...] = norm.reshape(chunk, padded, width)
    out = space + v_ref[9:10]
    d_norm = jnp.zeros_like(space)
    for block in range(blocks):
        cols = slice(block * width, (block + 1) * width)
        hidden = dot_nn(norm, w1_ref[:, cols]) + v_ref[10 + block : 11 + block]
        phi, density = gelu_parts(hidden)
        active = (hidden * phi).astype(BF)
        active_ref[:, :, cols] = active.reshape(chunk, padded, width)
        out += dot_nn(active, w2_ref[:, cols])
        d_hidden = dot_nt(cot, w2_ref[:, cols]) * (phi + hidden * density)
        vec_ref[3 + block : 4 + block] += col_sum(d_hidden.astype(BF).astype(F32))
        d_hidden = d_hidden.astype(BF)
        dhid_ref[:, :, cols] = d_hidden.reshape(chunk, padded, width)
        d_norm += dot_nt(d_hidden, w1_ref[:, cols])
    for frame in range(chunk):
        out_ref[frame] = out[frame * padded : frame * padded + places].astype(BF)
    vec_ref[0:1] += col_sum(d_norm * unit)
    vec_ref[1:2] += col_sum(d_norm)
    vec_ref[2:3] += col_sum(cot.astype(F32))
    grad = cot.astype(F32) + norm_back(unit, scale, v_ref[7:8], d_norm)
    grad_ref[...] = grad.reshape(chunk, padded, width)


def feed_grads(norm_ref, dhid_ref, active_ref, cot_ref, out_ref, norm_turned, cot_turned):
    width = norm_ref.shape[1]

    @pl.when(pl.program_id(0) == 0)
    def _():
        norm_turned[...] = norm_ref[...].T
        cot_turned[...] = cot_ref[...].T

    out_ref[:, :width] = dot_nn(norm_turned[...], dhid_ref[...]).astype(BF)
    out_ref[:, width:] = dot_nn(cot_turned[...], active_ref[...]).astype(BF).T


def spatial_back(places, grad_ref, after_ref, joined_ref, s_ref, v_ref, dspace_ref, djoin_ref, dat_ref, dtime_ref, vec_ref, dmix_ref):
    chunk, padded, width = grad_ref.shape

    @pl.when(pl.program_id(0) == 0)
    def _():
        vec_ref[...] = jnp.zeros_like(vec_ref)

    grad = rows_of(grad_ref[...])
    d_space = grad.astype(BF)
    dspace_ref[...] = d_space.reshape(chunk, padded, width)
    vec_ref[2:3] += col_sum(d_space.astype(F32))
    dmix_ref[...] = dot_nt(d_space, s_ref[:, 3 * width :]).astype(BF).reshape(chunk, padded, width)
    allowed = jnp.where(lax.broadcasted_iota(jnp.int32, (padded, 1), 0) < places, 0.0, LOW)
    for frame in range(chunk):
        for first in range(0, PAIRS, GROUP_SB):
            group = range(first, first + GROUP_SB)
            tiles = [
                [joined_ref[frame, :, pair_cols(i, pair, width)] for i in range(3)]
                + [dmix_ref[frame, :, pair_cols(0, pair, width)]]
                for pair in group
            ]
            for pair, grads in zip(group, heads_backward(tiles, allowed)):
                for i in range(3):
                    djoin_ref[frame, :, pair_cols(i, pair, width)] = grads[i]
    d_joined = rows_of(djoin_ref[...])
    d_norm = dot_nt(d_joined, s_ref[:, : 3 * width])
    unit, scale = normalize(rows_of(after_ref[...]))
    vec_ref[0:1] += col_sum(d_norm * unit)
    vec_ref[1:2] += col_sum(d_norm)
    d_time = grad + norm_back(unit, scale, v_ref[4:5], d_norm)
    dat_ref[...] = d_time.reshape(chunk, padded, width)
    dtime_ref[...] = d_time.astype(BF).reshape(chunk, padded, width)


def turned_grads(count, norm_ref, djoin_ref, *refs):
    i = pl.program_id(0)
    out_ref, norm_turned = refs[-2:]

    @pl.when(i == 0)
    def _():
        norm_turned[...] = norm_ref[...].T

    @pl.when(i < count)
    def _():
        out_ref[...] = dot_nn(norm_turned[...], djoin_ref[...]).astype(BF)

    if len(refs) > 2:

        @pl.when(i == count)
        def _():
            out_ref[...] = dot_tn(refs[0][...], refs[1][...]).astype(BF)


def temporal_back_project(dtime_ref, ol_ref, dproj_ref, dmix_ref, vec_ref):
    chunk, padded, width = dtime_ref.shape

    @pl.when(pl.program_id(0) == 0)
    def _():
        vec_ref[...] = jnp.zeros_like(vec_ref)

    d_time = rows_of(dtime_ref[...])
    vec_ref[1:2] += col_sum(d_time.astype(F32))
    d_proj = dot_nt(d_time, ol_ref[:, width:]).astype(BF)
    vec_ref[0:1] += col_sum(d_proj.astype(F32))
    dproj_ref[...] = d_proj.reshape(chunk, padded, width)
    dmix_ref[...] = dot_nt(d_proj, ol_ref[:, :width]).astype(BF).reshape(chunk, padded, width)


def temporal_back_attend(joined_ref, dmix_ref, djoin_ref):
    frames, tile, width = dmix_ref.shape
    bias = place_mask(frames * tile)
    for first in range(0, PAIRS, GROUP_TB):
        group = range(first, first + GROUP_TB)
        tiles = [
            [rows_of(joined_ref[:, :, pair_cols(i, pair, width)]) for i in range(3)]
            + [rows_of(dmix_ref[:, :, pair_cols(0, pair, width)])]
            for pair in group
        ]
        for pair, grads in zip(group, heads_backward(tiles, bias)):
            for i in range(3):
                djoin_ref[:, :, pair_cols(i, pair, width)] = grads[i].reshape(frames, tile, PAIR)


def temporal_back_finish(places, dat_ref, x_ref, djoin_ref, qk_ref, v_in_ref, v_ref, gx_ref, vec_ref):
    chunk, padded, width = x_ref.shape

    @pl.when(pl.program_id(0) == 0)
    def _():
        vec_ref[...] = jnp.zeros_like(vec_ref)

    d_joined = rows_of(djoin_ref[...])
    d_norm = dot_nt(d_joined[:, : 2 * width], qk_ref[...]) + dot_nt(d_joined[:, 2 * width :], v_in_ref[:, :width])
    d_norm = d_norm.astype(BF).astype(F32)
    unit, scale = normalize(rows_of(x_ref[...]).astype(F32))
    vec_ref[0:1] += col_sum(d_norm * unit)
    vec_ref[1:2] += col_sum(d_norm)
    grad = rows_of(dat_ref[...]) + norm_back(unit, scale, v_ref[0:1], d_norm)
    gx_ref[...] = grad.astype(BF).reshape(chunk, padded, width)[:, :places]


def whole(shape):
    return pl.BlockSpec(shape, lambda *i: (0,) * len(shape))


def cost(micros):
    return pl.CostEstimate(flops=int(micros * 1e9), bytes_accessed=0, transcendentals=0)


def params(mib=60):
    return pltpu.CompilerParams(vmem_limit_bytes=mib << 20)


def shape_of(*dims, dtype=BF):
    return jax.ShapeDtypeStruct(dims, dtype)


ANYWHERE = pl.BlockSpec(memory_space=pl.ANY)


def launch(kernel, micros, args, in_specs, out_specs, out_shape, grid, scratch=(), after=()):
    count, skip = len(args), len(after)

    def body(*refs):
        kernel(*refs[:count], *refs[count + skip :])

    return pl.pallas_call(
        body,
        grid=grid,
        in_specs=list(in_specs) + [ANYWHERE] * skip,
        out_specs=out_specs,
        out_shape=out_shape,
        scratch_shapes=list(scratch),
        cost_estimate=cost(micros),
        compiler_params=params(),
    )(*args, *after)


def gate(value, *after):
    def body(*refs):
        pass

    return pl.pallas_call(
        body,
        in_specs=[ANYWHERE] * (1 + len(after)),
        out_specs=ANYWHERE,
        out_shape=jax.ShapeDtypeStruct(value.shape, value.dtype),
        input_output_aliases={0: 0},
    )(value, *after)


def frame_block(chunk, padded, width):
    return pl.BlockSpec((chunk, padded, width), lambda i: (i, 0, 0))


def place_block(frames, width):
    return pl.BlockSpec((frames, TILE, width), lambda i: (0, i, 0))


def wholes(arrays):
    return [whole(a.shape) for a in arrays]


def flat(a):
    return a.reshape(-1, a.shape[-1])


def run_temporal_project(x, qk, v_in, v, chunk=2, after=()):
    frames, padded, width = x.shape
    block, wide = frame_block(chunk, padded, width), frame_block(chunk, padded, 3 * width)
    return launch(
        temporal_project, 9, (x, qk, v_in, v), [block] + wholes((qk, v_in, v)), [block, wide],
        (shape_of(*x.shape), shape_of(frames, padded, 3 * width)), (frames // chunk,), after=after,
    )


def run_temporal_attend(joined, after=()):
    frames, padded, wide = joined.shape
    width = wide // 3
    return launch(
        temporal_attend, 14, (joined,), [place_block(frames, wide)], place_block(frames, width),
        shape_of(frames, padded, width), (padded // TILE,), after=after,
    )


def run_temporal_finish(x, mixed, ol, v, chunk=2, after=()):
    frames, padded, width = x.shape
    block = frame_block(chunk, padded, width)
    return launch(
        temporal_finish, 8, (x, mixed, ol, v), [block, block] + wholes((ol, v)), [block, block],
        (shape_of(*x.shape), shape_of(*x.shape, dtype=F32)), (frames // chunk,), after=after,
    )


def run_spatial_forward(places, attended, pack, v, chunk=2, after=()):
    frames, padded, width = attended.shape
    block, wide = frame_block(chunk, padded, width), frame_block(chunk, padded, 3 * width)
    dims = attended.shape
    return launch(
        functools.partial(spatial_forward, places), 23, (attended, pack, v),
        [block, pl.BlockSpec((width, 4 * width), lambda i: (0, 2)), whole(v.shape)],
        [block, wide, block, block],
        (shape_of(*dims), shape_of(frames, padded, 3 * width), shape_of(*dims), shape_of(*dims, dtype=F32)),
        (frames // chunk,), after=after,
    )


def run_feed(places, space, cot, pack, v, chunk=2, after=()):
    frames, padded, width = space.shape
    hidden = 4 * width
    block, wide = frame_block(chunk, padded, width), frame_block(chunk, padded, hidden)
    dims = space.shape
    return launch(
        functools.partial(feed_both, places), 45, (space, cot, pack, pack, v),
        [
            block, block,
            pl.BlockSpec((width, hidden), lambda i: (0, 0)),
            pl.BlockSpec((width, hidden), lambda i: (0, 1)),
            whole(v.shape),
        ],
        [frame_block(chunk, places, width), block, block, wide, wide, whole((8, width))],
        (
            shape_of(frames, places, width), shape_of(*dims, dtype=F32), shape_of(*dims),
            shape_of(frames, padded, hidden), shape_of(frames, padded, hidden), shape_of(8, width, dtype=F32),
        ),
        (frames // chunk,), after=after,
    )


def run_feed_grads(norm, d_hidden, active, cot, after=()):
    norm, d_hidden, active, cot = flat(norm), flat(d_hidden), flat(active), flat(cot)
    rows, width = norm.shape
    blocks = d_hidden.shape[1] // width
    part = pl.BlockSpec((rows, width), lambda i: (0, i))
    return launch(
        feed_grads, 25, (norm, d_hidden, active, cot), [whole((rows, width)), part, part, whole((rows, width))],
        pl.BlockSpec((width, 2 * width), lambda i: (0, i)), shape_of(width, 2 * width * blocks), (blocks,),
        scratch=[pltpu.VMEM((width, rows), BF), pltpu.VMEM((width, rows), BF)], after=after,
    )


def run_spatial_back(places, grad, attended, joined, pack, v, chunk=2, after=()):
    frames, padded, width = grad.shape
    block, wide = frame_block(chunk, padded, width), frame_block(chunk, padded, 3 * width)
    dims = grad.shape
    return launch(
        functools.partial(spatial_back, places), 42, (grad, attended, joined, pack, v),
        [block, block, wide, pl.BlockSpec((width, 4 * width), lambda i: (0, 2)), whole(v.shape)],
        [block, wide, block, block, whole((8, width))],
        (
            shape_of(*dims), shape_of(frames, padded, 3 * width), shape_of(*dims, dtype=F32), shape_of(*dims),
            shape_of(8, width, dtype=F32),
        ),
        (frames // chunk,), scratch=[pltpu.VMEM((chunk, padded, width), BF)], after=after,
    )


def run_join_grads(norm, d_joined, *more, after=()):
    norm, d_joined = flat(norm), flat(d_joined)
    more = [flat(a) for a in more]
    rows, width = norm.shape
    count = d_joined.shape[1] // width
    steps = count + (1 if more else 0)
    return launch(
        functools.partial(turned_grads, count), 4 * steps, (norm, d_joined, *more),
        [whole((rows, width)), pl.BlockSpec((rows, width), lambda i: (0, jnp.minimum(i, count - 1)))] + wholes(more),
        pl.BlockSpec((width, width), lambda i: (0, i)), shape_of(width, steps * width), (steps,),
        scratch=[pltpu.VMEM((width, rows), BF)], after=after,
    )


def feed_out(n, g_ref, w1_ref, w2_ref):
    rows, hidden = w1_ref.shape
    width = w2_ref.shape[1]
    parts = hidden // width
    for j in range(parts):
        block = g_ref[:, 2 * j * width : (2 * j + 1) * width].astype(F32)
        for i in range(n):
            at = (i * parts + j) * rows
            w1_ref[:, at : at + rows] = block[:, i * rows : (i + 1) * rows]
        w2_ref[j * rows : (j + 1) * rows] = g_ref[:, (2 * j + 1) * width : (2 * j + 2) * width].astype(F32)


def run_feed_out(g, n):
    rows = g.shape[0]
    width = rows * n
    parts = g.shape[1] // (2 * width)
    outs = (shape_of(rows, parts * width, dtype=F32), shape_of(parts * rows, width, dtype=F32))
    return pl.pallas_call(
        functools.partial(feed_out, n), out_shape=outs, cost_estimate=cost(3), compiler_params=params()
    )(g)


def tile_grad(a_ref, b_ref, out_ref):
    out_ref[...] = dot_tn(a_ref[...], b_ref[...]).astype(BF)


def run_tile_grad(a, b, after=()):
    a, b = flat(a), flat(b)
    rows, width = a.shape
    return launch(
        tile_grad, 6, (a, b), [pl.BlockSpec((rows, width // 2), lambda i: (0, i)), whole(b.shape)],
        pl.BlockSpec((width // 2, b.shape[1]), lambda i: (i, 0)), shape_of(width, b.shape[1]), (2,), after=after,
    )


def run_temporal_back_project(d_time, ol, chunk=2, after=()):
    frames, padded, width = d_time.shape
    block = frame_block(chunk, padded, width)
    dims = d_time.shape
    return launch(
        temporal_back_project, 8, (d_time, ol), [block, whole(ol.shape)], [block, block, whole((8, width))],
        (shape_of(*dims), shape_of(*dims), shape_of(8, width, dtype=F32)), (frames // chunk,), after=after,
    )


def run_temporal_back_attend(joined, d_mixed, after=()):
    frames, padded, width = d_mixed.shape
    wide = place_block(frames, 3 * width)
    return launch(
        temporal_back_attend, 20, (joined, d_mixed), [wide, place_block(frames, width)], wide,
        shape_of(frames, padded, 3 * width), (padded // TILE,), after=after,
    )


def run_temporal_back_finish(places, d_at, x, d_joined, qk, v_in, v, chunk=2, after=()):
    frames, padded, width = x.shape
    block, wide = frame_block(chunk, padded, width), frame_block(chunk, padded, 3 * width)
    return launch(
        functools.partial(temporal_back_finish, places), 11, (d_at, x, d_joined, qk, v_in, v),
        [block, block, wide] + wholes((qk, v_in, v)), [frame_block(chunk, places, width), whole((8, width))],
        (shape_of(frames, places, width), shape_of(8, width, dtype=F32)), (frames // chunk,), after=after,
    )


AXES = ("dp", "seq")


def swap(values, bit, n):
    return lax.ppermute(values, AXES, [(i, i ^ (1 << bit)) for i in range(n)])


class Gather:
    def __init__(self, values, n, order):
        self.n, self.bits, self.order = n, n.bit_length() - 1, list(order)
        self.me = lax.axis_index(AXES)
        self.tail = values.shape[1:]
        self.held = values.reshape((1,) * self.bits + values.shape)

    def start(self):
        self.bit = self.order.pop(0)
        self.got = swap(self.held, self.bit, self.n)
        return self.held

    def end(self, *after):
        got = gate(self.got, *after) if after else self.got
        axis = self.bits - 1 - self.bit
        high = ((self.me >> self.bit) & 1) == 1
        held = self.held
        self.held = jnp.where(high, jnp.concatenate([got, held], axis), jnp.concatenate([held, got], axis))

    def steps(self, count):
        for _ in range(count):
            self.start()
            self.end()

    def rest(self):
        self.steps(len(self.order))
        return self.result()

    def result(self):
        return self.held.reshape((-1,) + self.tail)


class Scatter:
    def __init__(self, values, n, order):
        self.n, self.bits, self.order = n, n.bit_length() - 1, list(order)
        self.rows, self.tail = values.shape[0] // n, values.shape[1:]
        self.me = lax.axis_index(AXES)
        self.held = values.reshape((2,) * self.bits + (self.rows,) + self.tail)

    def start(self):
        bit = self.order.pop(0)
        axis = self.bits - 1 - bit
        mine = (self.me >> bit) & 1
        send = lax.dynamic_index_in_dim(self.held, 1 - mine, axis, keepdims=True)
        self.keep = lax.dynamic_index_in_dim(self.held, mine, axis, keepdims=True)
        self.got = swap(send, bit, self.n)
        return send

    def end(self, *after):
        got = gate(self.got, *after) if after else self.got
        self.held = (self.keep.astype(F32) + got.astype(F32)).astype(self.held.dtype)

    def rest(self, *after):
        while self.order:
            self.start()
            self.end(*(() if self.order else after))
        return self.result()

    def result(self):
        return self.held.reshape((self.rows,) + self.tail)


def on_device(n, tokens, tg, tb, t_in, t_out, t_lin, sg, sb, s_in, s_out, fg, fb, w1, b1, w2, cotangent):
    bits = n.bit_length() - 1
    top = tuple(range(bits - 1, 2, -1))
    order_a, order_b, order_c = top + (1, 2, 0), top + (2, 1, 0), (2,) + top + (1, 0)
    back_y, back_z = (0, 2) + top[::-1] + (1,), (0,) + top[::-1] + (2, 1)
    rows, width = t_in.shape[0], t_in.shape[0] * n
    parts = w2.shape[0] // rows
    hidden = w1.shape[1]
    places = tokens.shape[2]
    frames = tokens.shape[0] * tokens.shape[1]
    extra = -places % TILE

    vecs = jnp.concatenate([tg[None], tb, sg[None], sb, fg[None], fb, b1.reshape(parts, rows)], axis=0)
    n_vec = vecs.shape[0]
    vec_cols = jnp.pad(vecs.T, ((0, 0), (0, 2 * HEAD_DIM - n_vec)))
    feed = jnp.concatenate(
        [
            w1.reshape(rows, n, parts, rows).transpose(0, 2, 1, 3).reshape(rows, hidden),
            w2.reshape(parts, rows, width).transpose(1, 0, 2).reshape(rows, hidden),
            s_in,
            s_out,
        ],
        axis=1,
    )
    feed = lax.all_gather(feed, AXES, axis=0, tiled=True)

    def own_clip(grid):
        clip = lax.all_to_all(grid, "seq", split_axis=0, concat_axis=0, tiled=True)
        return jnp.pad(clip.reshape(frames, places, width), ((0, 0), (0, extra), (0, 0)))

    def own_frames(clip):
        return lax.all_to_all(clip.reshape(tokens.shape), "seq", split_axis=0, concat_axis=0, tiled=True)

    x = own_clip(tokens)
    t_qk = Gather(t_in[:, : 2 * width], n, order_a)
    t_v = Gather(jnp.concatenate([t_in[:, 2 * width :], vec_cols], axis=1), n, order_c)
    t_ol = Gather(jnp.concatenate([t_out, t_lin], axis=1), n, order_b)
    t_qk_w, t_v_w = t_qk.rest(), t_v.rest()
    t_ol.steps(bits - 1)
    vec = t_v_w[:, width:].T[:16].astype(F32)
    norm_t, joined_t = run_temporal_project(x, t_qk_w, t_v_w, vec, after=(t_ol.start(),))
    t_ol.end(norm_t)
    t_ol_w = t_ol.result()
    mixed_t = run_temporal_attend(joined_t)
    proj_t, after_time = run_temporal_finish(x, mixed_t, t_ol_w, vec)
    cot = own_clip(gate(cotangent, norm_t))
    norm_s, joined_s, mixed_s, after_space = run_spatial_forward(places, after_time, feed, vec)
    out, d_after_space, norm_m, active, d_hidden, vec_f = run_feed(places, after_space, cot, feed, vec)
    output = own_frames(out)
    g_feed_all = run_feed_grads(norm_m, d_hidden, active, cot)
    g_feed = lax.psum_scatter(g_feed_all, AXES, scatter_dimension=0, tiled=True)
    o_w1, o_w2 = run_feed_out(g_feed, n)
    d_space, d_joined_s, d_after_time, d_time, vec_s = run_spatial_back(
        places, d_after_space, after_time, joined_s, feed, vec, after=(g_feed_all,)
    )
    g_space = run_join_grads(norm_s, d_joined_s, mixed_s, d_space, after=(output[0, :1, 0, :128],))

    def beside(chains, kernel, *args):
        sends = tuple(chain.start() for chain in chains)
        done = kernel(*args, after=sends)
        for chain in chains:
            chain.end(done[0] if isinstance(done, (tuple, list)) else done)
        return done

    gs = Scatter(g_space, n, order_a[::-1])
    g_lin = beside((gs,), run_tile_grad, proj_t, d_time)
    d_proj, d_mixed_t, vec_t1 = beside((gs,), run_temporal_back_project, d_time, t_ol_w)
    g_out = run_tile_grad(mixed_t, d_proj)
    go = Scatter(jnp.concatenate([g_out, g_lin], axis=1), n, order_b[::-1])
    d_joined_t = beside((gs, go), run_temporal_back_attend, joined_t, d_mixed_t)
    g_qkv = beside((gs, go), run_join_grads, norm_t, d_joined_t)
    half = 3 * width // 2
    gq, gr = Scatter(g_qkv[:, :half], n, back_y), Scatter(g_qkv[:, half:], n, back_z)
    g_x, vec_t0 = beside(
        (gs, go, gq, gr), run_temporal_back_finish, places, d_after_time, x, d_joined_t, t_qk_w, t_v_w, vec
    )
    g_x = own_frames(g_x)
    g_vec = jnp.concatenate([vec_t0[:2], vec_t1[:2], vec_s[:3], vec_f[: 3 + parts]], axis=0)
    g_vec = g_vec.reshape(n_vec, n, rows).transpose(1, 0, 2)
    v = jnp.sum(lax.all_to_all(g_vec, AXES, split_axis=0, concat_axis=0, tiled=True), axis=0)
    g_i = jnp.concatenate([gq.rest(), gr.rest(o_w1[:1, :128])], axis=1).astype(F32)
    g_s = gs.rest().astype(F32)
    g_o = go.rest().astype(F32)
    return (
        output, g_x, v[0], v[1:4], g_i, g_o[:, :width], g_o[:, width : 2 * width],
        v[4], v[5:7], g_s[:, : 3 * width], g_s[:, 3 * width :], v[7], v[8:10],
        o_w1, v[10 : 10 + parts].reshape(-1), o_w2,
    )


def solution(mesh):
    shard = P(("dp", "seq"))
    cols = P(None, ("dp", "seq"))
    mat = P(("dp", "seq"), None)
    tok = P("dp", "seq", None, None)
    in_specs = (tok, shard, cols, mat, mat, mat, shard, cols, mat, mat, shard, cols, mat, shard, mat, tok)
    out_specs = (tok, tok, shard, cols, mat, mat, mat, shard, cols, mat, mat, shard, cols, mat, shard, mat)
    return jax.shard_map(
        functools.partial(on_device, mesh.size), mesh=mesh, in_specs=in_specs, out_specs=out_specs, check_vma=False
    )
```

```python
import functools

import jax
import jax.numpy as jnp
from jax import lax
from jax.experimental import pallas as pl
from jax.experimental.pallas import tpu as pltpu
from jax.sharding import PartitionSpec as P

HEADS = 12
HEAD_DIM = 64
PAIR = 2 * HEAD_DIM
PAIRS = HEADS // 2
TILE = 16
GROUP_T = 6
GROUP_S = 2
GROUP_SB = 1
GROUP_TB = 3
LOW = -1e30
BF = jnp.bfloat16
F32 = jnp.float32


def dot_nn(a, b):
    return lax.dot_general(a, b, (((1,), (0,)), ((), ())), preferred_element_type=F32)


def dot_nt(a, b):
    return lax.dot_general(a, b, (((1,), (1,)), ((), ())), preferred_element_type=F32)


def dot_tn(a, b):
    return lax.dot_general(a, b, (((0,), (0,)), ((), ())), preferred_element_type=F32)


def normalize(values):
    center = values - jnp.mean(values, axis=-1, keepdims=True)
    scale = lax.rsqrt(jnp.mean(center * center, axis=-1, keepdims=True) + 1e-05)
    return center * scale, scale


def norm_back(unit, scale, gain, grad):
    graded = grad * gain
    shift = jnp.mean(graded, axis=-1, keepdims=True)
    slope = jnp.mean(graded * unit, axis=-1, keepdims=True)
    return scale * (graded - shift - unit * slope)


def rows_of(block):
    return block.reshape(block.shape[0] * block.shape[1], block.shape[2])


def col_sum(values):
    return jnp.sum(values, axis=0, keepdims=True)


def lane_halves(shape):
    return lax.broadcasted_iota(jnp.int32, shape, len(shape) - 1) < HEAD_DIM


def half_masks():
    low_half = lane_halves((1, PAIR))
    return (
        jnp.where(low_half, 1.0, 0.0).astype(BF),
        jnp.where(low_half, 0.0, 1.0).astype(BF),
    )


def heads_forward(tiles, bias):
    low_mask, high_mask = half_masks()
    scale = HEAD_DIM ** (-0.5)
    scores = []
    for query, key, value in tiles:
        for mask in (low_mask, high_mask):
            scores.append(dot_nt(query * (mask * scale), key) + bias)
    tops = [jnp.max(s, axis=-1, keepdims=True) for s in scores]
    shares = [jnp.exp(s - top).astype(BF) for s, top in zip(scores, tops)]
    outs = []
    for at, share in enumerate(shares):
        value = tiles[at // 2][2]
        outs.append(dot_nn(share, jnp.concatenate([value, jnp.ones_like(value)], axis=1)))
    mixed = []
    for at in range(len(tiles)):
        first, second = outs[2 * at], outs[2 * at + 1]
        low_half = lane_halves((first.shape[0], PAIR))
        top = jnp.where(low_half, first[:, :PAIR], second[:, :PAIR])
        total = jnp.where(low_half, first[:, PAIR:], second[:, PAIR:])
        mixed.append((top / total).astype(BF))
    return mixed


def heads_backward(tiles, bias):
    low_mask, high_mask = half_masks()
    scale = HEAD_DIM ** (-0.5)
    turned = [key.T for query, key, value, grad in tiles]
    queries, grads, scores, grad_shares = [], [], [], []
    for query, key, value, grad in tiles:
        for mask in (low_mask, high_mask):
            queries.append(query * (mask * scale))
            grads.append(grad * mask)
            scores.append(dot_nt(key, queries[-1]) + bias)
            grad_shares.append(dot_nt(value, grads[-1]))
    tops = [jnp.max(s, axis=0, keepdims=True) for s in scores]
    raw = [jnp.exp(s - top) for s, top in zip(scores, tops)]
    inverse = [1.0 / jnp.sum(e, axis=0, keepdims=True) for e in raw]
    shares = [e * i for e, i in zip(raw, inverse)]
    terms = [jnp.sum(g * p, axis=0, keepdims=True) for g, p in zip(grad_shares, shares)]
    grad_scores = [(p * (g - t)).astype(BF) for p, g, t in zip(shares, grad_shares, terms)]
    shares = [p.astype(BF) for p in shares]
    out = []
    for at in range(len(tiles)):
        a, b = 2 * at, 2 * at + 1
        grad_value = dot_nn(shares[a], grads[a]) + dot_nn(shares[b], grads[b])
        grad_key = dot_nn(grad_scores[a], queries[a]) + dot_nn(grad_scores[b], queries[b])
        key_turned = turned[at]
        grad_query = jnp.concatenate(
            [dot_nn(key_turned[:HEAD_DIM], grad_scores[a]), dot_nn(key_turned[HEAD_DIM:], grad_scores[b])], axis=0
        )
        out.append(((grad_query * scale).astype(BF).T, grad_key.astype(BF), grad_value.astype(BF)))
    return out


def place_mask(size):
    row = lax.broadcasted_iota(jnp.int32, (size, size), 0)
    col = lax.broadcasted_iota(jnp.int32, (size, size), 1)
    return jnp.where(((row ^ col) & (TILE - 1)) == 0, 0.0, LOW)


def pair_cols(part, pair, width):
    start = part * width + pair * PAIR
    return slice(start, start + PAIR)


def temporal_project(x_ref, qk_ref, v_in_ref, v_ref, norm_ref, joined_ref):
    chunk, padded, width = x_ref.shape
    unit, scale = normalize(rows_of(x_ref[...]).astype(F32))
    norm = (unit * v_ref[0:1] + v_ref[1:2]).astype(BF)
    norm_ref[...] = norm.reshape(chunk, padded, width)
    for part in range(3):
        cols = slice(part * width, (part + 1) * width)
        weight = qk_ref[:, cols] if part < 2 else v_in_ref[:, :width]
        joined_ref[:, :, cols] = dot_nn(norm, weight).astype(BF).reshape(chunk, padded, width)


def temporal_attend(joined_ref, mixed_ref):
    frames, tile, width = mixed_ref.shape
    bias = place_mask(frames * tile)
    for first in range(0, PAIRS, GROUP_T):
        group = range(first, first + GROUP_T)
        tiles = [[rows_of(joined_ref[:, :, pair_cols(i, pair, width)]) for i in range(3)] for pair in group]
        for pair, mixed in zip(group, heads_forward(tiles, bias)):
            mixed_ref[:, :, pair_cols(0, pair, width)] = mixed.reshape(frames, tile, PAIR)


def temporal_finish(x_ref, mixed_ref, ol_ref, v_ref, proj_ref, after_ref):
    chunk, padded, width = x_ref.shape
    proj = (dot_nn(rows_of(mixed_ref[...]), ol_ref[:, :width]) + v_ref[2:3]).astype(BF)
    proj_ref[...] = proj.reshape(chunk, padded, width)
    branch = (dot_nn(proj, ol_ref[:, width:]) + v_ref[3:4]).astype(BF)
    after = rows_of(x_ref[...]).astype(F32) + branch.astype(F32)
    after_ref[...] = after.reshape(chunk, padded, width)


def spatial_forward(places, after_ref, s_ref, v_ref, norm_ref, joined_ref, mixed_ref, space_ref):
    chunk, padded, width = after_ref.shape
    after = rows_of(after_ref[...])
    unit, scale = normalize(after)
    norm = (unit * v_ref[4:5] + v_ref[5:6]).astype(BF)
    norm_ref[...] = norm.reshape(chunk, padded, width)
    for part in range(3):
        cols = slice(part * width, (part + 1) * width)
        joined_ref[:, :, cols] = dot_nn(norm, s_ref[:, cols]).astype(BF).reshape(chunk, padded, width)
    allowed = jnp.where(lax.broadcasted_iota(jnp.int32, (1, padded), 1) < places, 0.0, LOW)
    for frame in range(chunk):
        for first in range(0, PAIRS, GROUP_S):
            group = range(first, first + GROUP_S)
            tiles = [[joined_ref[frame, :, pair_cols(i, pair, width)] for i in range(3)] for pair in group]
            for pair, mixed in zip(group, heads_forward(tiles, allowed)):
                mixed_ref[frame, :, pair_cols(0, pair, width)] = mixed
    space = after + dot_nn(rows_of(mixed_ref[...]), s_ref[:, 3 * width :]) + v_ref[6:7]
    space_ref[...] = space.reshape(chunk, padded, width)


def gelu_parts(hidden):
    phi = 0.5 * (1.0 + lax.erf(hidden * 0.7071067811865476))
    density = jnp.exp(-0.5 * hidden * hidden) * 0.3989422804014327
    return phi, density


def feed_both(places, space_ref, cot_ref, w1_ref, w2_ref, v_ref, out_ref, grad_ref, norm_ref, active_ref, dhid_ref, vec_ref):
    chunk, padded, width = space_ref.shape
    blocks = w1_ref.shape[1] // width

    @pl.when(pl.program_id(0) == 0)
    def _():
        vec_ref[...] = jnp.zeros_like(vec_ref)

    space = rows_of(space_ref[...])
    cot = rows_of(cot_ref[...])
    unit, scale = normalize(space)
    norm = (unit * v_ref[7:8] + v_ref[8:9]).astype(BF)
    norm_ref[...] = norm.reshape(chunk, padded, width)
    out = space + v_ref[9:10]
    d_norm = jnp.zeros_like(space)
    for block in range(blocks):
        cols = slice(block * width, (block + 1) * width)
        hidden = dot_nn(norm, w1_ref[:, cols]) + v_ref[10 + block : 11 + block]
        phi, density = gelu_parts(hidden)
        active = (hidden * phi).astype(BF)
        active_ref[:, :, cols] = active.reshape(chunk, padded, width)
        out += dot_nn(active, w2_ref[:, cols])
        d_hidden = dot_nt(cot, w2_ref[:, cols]) * (phi + hidden * density)
        vec_ref[3 + block : 4 + block] += col_sum(d_hidden.astype(BF).astype(F32))
        d_hidden = d_hidden.astype(BF)
        dhid_ref[:, :, cols] = d_hidden.reshape(chunk, padded, width)
        d_norm += dot_nt(d_hidden, w1_ref[:, cols])
    for frame in range(chunk):
        out_ref[frame] = out[frame * padded : frame * padded + places].astype(BF)
    vec_ref[0:1] += col_sum(d_norm * unit)
    vec_ref[1:2] += col_sum(d_norm)
    vec_ref[2:3] += col_sum(cot.astype(F32))
    grad = cot.astype(F32) + norm_back(unit, scale, v_ref[7:8], d_norm)
    grad_ref[...] = grad.reshape(chunk, padded, width)


def feed_grads(norm_ref, dhid_ref, active_ref, cot_ref, out_ref, norm_turned, cot_turned):
    width = norm_ref.shape[1]

    @pl.when(pl.program_id(0) == 0)
    def _():
        norm_turned[...] = norm_ref[...].T
        cot_turned[...] = cot_ref[...].T

    out_ref[:, :width] = dot_nn(norm_turned[...], dhid_ref[...]).astype(BF)
    out_ref[:, width:] = dot_nn(cot_turned[...], active_ref[...]).astype(BF).T


def spatial_back(places, grad_ref, after_ref, joined_ref, s_ref, v_ref, dspace_ref, djoin_ref, dat_ref, dtime_ref, vec_ref, dmix_ref):
    chunk, padded, width = grad_ref.shape

    @pl.when(pl.program_id(0) == 0)
    def _():
        vec_ref[...] = jnp.zeros_like(vec_ref)

    grad = rows_of(grad_ref[...])
    d_space = grad.astype(BF)
    dspace_ref[...] = d_space.reshape(chunk, padded, width)
    vec_ref[2:3] += col_sum(d_space.astype(F32))
    dmix_ref[...] = dot_nt(d_space, s_ref[:, 3 * width :]).astype(BF).reshape(chunk, padded, width)
    allowed = jnp.where(lax.broadcasted_iota(jnp.int32, (padded, 1), 0) < places, 0.0, LOW)
    for frame in range(chunk):
        for first in range(0, PAIRS, GROUP_SB):
            group = range(first, first + GROUP_SB)
            tiles = [
                [joined_ref[frame, :, pair_cols(i, pair, width)] for i in range(3)]
                + [dmix_ref[frame, :, pair_cols(0, pair, width)]]
                for pair in group
            ]
            for pair, grads in zip(group, heads_backward(tiles, allowed)):
                for i in range(3):
                    djoin_ref[frame, :, pair_cols(i, pair, width)] = grads[i]
    d_joined = rows_of(djoin_ref[...])
    d_norm = dot_nt(d_joined, s_ref[:, : 3 * width])
    unit, scale = normalize(rows_of(after_ref[...]))
    vec_ref[0:1] += col_sum(d_norm * unit)
    vec_ref[1:2] += col_sum(d_norm)
    d_time = grad + norm_back(unit, scale, v_ref[4:5], d_norm)
    dat_ref[...] = d_time.reshape(chunk, padded, width)
    dtime_ref[...] = d_time.astype(BF).reshape(chunk, padded, width)


def turned_grads(count, norm_ref, djoin_ref, *refs):
    i = pl.program_id(0)
    out_ref, norm_turned = refs[-2:]

    @pl.when(i == 0)
    def _():
        norm_turned[...] = norm_ref[...].T

    @pl.when(i < count)
    def _():
        out_ref[...] = dot_nn(norm_turned[...], djoin_ref[...]).astype(BF)

    if len(refs) > 2:

        @pl.when(i == count)
        def _():
            out_ref[...] = dot_tn(refs[0][...], refs[1][...]).astype(BF)


def temporal_back_project(dtime_ref, ol_ref, dproj_ref, dmix_ref, vec_ref):
    chunk, padded, width = dtime_ref.shape

    @pl.when(pl.program_id(0) == 0)
    def _():
        vec_ref[...] = jnp.zeros_like(vec_ref)

    d_time = rows_of(dtime_ref[...])
    vec_ref[1:2] += col_sum(d_time.astype(F32))
    d_proj = dot_nt(d_time, ol_ref[:, width:]).astype(BF)
    vec_ref[0:1] += col_sum(d_proj.astype(F32))
    dproj_ref[...] = d_proj.reshape(chunk, padded, width)
    dmix_ref[...] = dot_nt(d_proj, ol_ref[:, :width]).astype(BF).reshape(chunk, padded, width)


def temporal_back_attend(joined_ref, dmix_ref, djoin_ref):
    frames, tile, width = dmix_ref.shape
    bias = place_mask(frames * tile)
    for first in range(0, PAIRS, GROUP_TB):
        group = range(first, first + GROUP_TB)
        tiles = [
            [rows_of(joined_ref[:, :, pair_cols(i, pair, width)]) for i in range(3)]
            + [rows_of(dmix_ref[:, :, pair_cols(0, pair, width)])]
            for pair in group
        ]
        for pair, grads in zip(group, heads_backward(tiles, bias)):
            for i in range(3):
                djoin_ref[:, :, pair_cols(i, pair, width)] = grads[i].reshape(frames, tile, PAIR)


def temporal_back_finish(
    places, me_ref, dat_ref, x_ref, djoin_ref, qk_ref, v_in_ref, v_ref, vec_t_ref, vec_s_ref, vec_f_ref,
    gx_ref, turned_ref, vec_ref,
):
    chunk, padded, width = x_ref.shape

    @pl.when(pl.program_id(0) == 0)
    def _():
        vec_ref[...] = jnp.zeros_like(vec_ref)
        vec_ref[2:4] = vec_t_ref[0:2]
        vec_ref[4:7] = vec_s_ref[0:3]
        vec_ref[7:14] = vec_f_ref[0:7]

    d_joined = rows_of(djoin_ref[...])
    d_norm = dot_nt(d_joined[:, : 2 * width], qk_ref[...]) + dot_nt(d_joined[:, 2 * width :], v_in_ref[:, :width])
    d_norm = d_norm.astype(BF).astype(F32)
    unit, scale = normalize(rows_of(x_ref[...]).astype(F32))
    vec_ref[0:1] += col_sum(d_norm * unit)
    vec_ref[1:2] += col_sum(d_norm)
    grad = rows_of(dat_ref[...]) + norm_back(unit, scale, v_ref[0:1], d_norm)
    gx_ref[...] = grad.astype(BF).reshape(chunk, padded, width)[:, :places]

    @pl.when(pl.program_id(0) == pl.num_programs(0) - 1)
    def _():
        turned_ref[...] = vec_ref[...].T.astype(BF)


def whole(shape):
    return pl.BlockSpec(shape, lambda *i: (0,) * len(shape))


def cost(micros):
    return pl.CostEstimate(flops=int(micros * 1e8), bytes_accessed=0, transcendentals=0)


def params(mib=60):
    return pltpu.CompilerParams(vmem_limit_bytes=mib << 20)


def shape_of(*dims, dtype=BF):
    return jax.ShapeDtypeStruct(dims, dtype)


ANYWHERE = pl.BlockSpec(memory_space=pl.ANY)


def launch(kernel, micros, args, in_specs, out_specs, out_shape, grid, scratch=(), after=()):
    count, skip = len(args), len(after)

    def body(*refs):
        kernel(*refs[:count], *refs[count + skip :])

    return pl.pallas_call(
        body,
        grid=grid,
        in_specs=list(in_specs) + [ANYWHERE] * skip,
        out_specs=out_specs,
        out_shape=out_shape,
        scratch_shapes=list(scratch),
        cost_estimate=cost(micros),
        compiler_params=params(),
    )(*args, *after)


def gate(value, *after):
    return lax.optimization_barrier((value,) + after)[0]


def frame_block(chunk, padded, width):
    return pl.BlockSpec((chunk, padded, width), lambda i: (i, 0, 0))


def place_block(frames, width):
    return pl.BlockSpec((frames, TILE, width), lambda i: (0, i, 0))


def wholes(arrays):
    return [whole(a.shape) for a in arrays]


def flat(a):
    return a.reshape(-1, a.shape[-1])


def run_temporal_project(x, qk, v_in, v, chunk=2, after=()):
    frames, padded, width = x.shape
    block, wide = frame_block(chunk, padded, width), frame_block(chunk, padded, 3 * width)
    return launch(
        temporal_project, 9, (x, qk, v_in, v), [block] + wholes((qk, v_in, v)), [block, wide],
        (shape_of(*x.shape), shape_of(frames, padded, 3 * width)), (frames // chunk,), after=after,
    )


def run_temporal_attend(joined, after=()):
    frames, padded, wide = joined.shape
    width = wide // 3
    return launch(
        temporal_attend, 14, (joined,), [place_block(frames, wide)], place_block(frames, width),
        shape_of(frames, padded, width), (padded // TILE,), after=after,
    )


def run_temporal_finish(x, mixed, ol, v, chunk=2, after=()):
    frames, padded, width = x.shape
    block = frame_block(chunk, padded, width)
    return launch(
        temporal_finish, 8, (x, mixed, ol, v), [block, block] + wholes((ol, v)), [block, block],
        (shape_of(*x.shape), shape_of(*x.shape, dtype=F32)), (frames // chunk,), after=after,
    )


def run_spatial_forward(places, attended, pack, v, chunk=2, after=()):
    frames, padded, width = attended.shape
    block, wide = frame_block(chunk, padded, width), frame_block(chunk, padded, 3 * width)
    dims = attended.shape
    return launch(
        functools.partial(spatial_forward, places), 23, (attended, pack, v),
        [block, pl.BlockSpec((width, 4 * width), lambda i: (0, 2)), whole(v.shape)],
        [block, wide, block, block],
        (shape_of(*dims), shape_of(frames, padded, 3 * width), shape_of(*dims), shape_of(*dims, dtype=F32)),
        (frames // chunk,), after=after,
    )


def run_feed(places, space, cot, pack, v, chunk=2, after=()):
    frames, padded, width = space.shape
    hidden = 4 * width
    block, wide = frame_block(chunk, padded, width), frame_block(chunk, padded, hidden)
    dims = space.shape
    return launch(
        functools.partial(feed_both, places), 45, (space, cot, pack, pack, v),
        [
            block, block,
            pl.BlockSpec((width, hidden), lambda i: (0, 0)),
            pl.BlockSpec((width, hidden), lambda i: (0, 1)),
            whole(v.shape),
        ],
        [frame_block(chunk, places, width), block, block, wide, wide, whole((8, width))],
        (
            shape_of(frames, places, width), shape_of(*dims, dtype=F32), shape_of(*dims),
            shape_of(frames, padded, hidden), shape_of(frames, padded, hidden), shape_of(8, width, dtype=F32),
        ),
        (frames // chunk,), after=after,
    )


def run_feed_grads(norm, d_hidden, active, cot, after=()):
    norm, d_hidden, active, cot = flat(norm), flat(d_hidden), flat(active), flat(cot)
    rows, width = norm.shape
    blocks = d_hidden.shape[1] // width
    part = pl.BlockSpec((rows, width), lambda i: (0, i))
    return launch(
        feed_grads, 25, (norm, d_hidden, active, cot), [whole((rows, width)), part, part, whole((rows, width))],
        pl.BlockSpec((width, 2 * width), lambda i: (0, i)), shape_of(width, 2 * width * blocks), (blocks,),
        scratch=[pltpu.VMEM((width, rows), BF), pltpu.VMEM((width, rows), BF)], after=after,
    )


def run_spatial_back(places, grad, attended, joined, pack, v, chunk=2, after=()):
    frames, padded, width = grad.shape
    block, wide = frame_block(chunk, padded, width), frame_block(chunk, padded, 3 * width)
    dims = grad.shape
    return launch(
        functools.partial(spatial_back, places), 42, (grad, attended, joined, pack, v),
        [block, block, wide, pl.BlockSpec((width, 4 * width), lambda i: (0, 2)), whole(v.shape)],
        [block, wide, block, block, whole((8, width))],
        (
            shape_of(*dims), shape_of(frames, padded, 3 * width), shape_of(*dims, dtype=F32), shape_of(*dims),
            shape_of(8, width, dtype=F32),
        ),
        (frames // chunk,), scratch=[pltpu.VMEM((chunk, padded, width), BF)], after=after,
    )


def run_join_grads(norm, d_joined, *more, after=()):
    norm, d_joined = flat(norm), flat(d_joined)
    more = [flat(a) for a in more]
    rows, width = norm.shape
    count = d_joined.shape[1] // width
    steps = count + (1 if more else 0)
    return launch(
        functools.partial(turned_grads, count), 4 * steps, (norm, d_joined, *more),
        [whole((rows, width)), pl.BlockSpec((rows, width), lambda i: (0, jnp.minimum(i, count - 1)))] + wholes(more),
        pl.BlockSpec((width, width), lambda i: (0, i)), shape_of(width, steps * width), (steps,),
        scratch=[pltpu.VMEM((width, rows), BF)], after=after,
    )


def feed_out(n, g_ref, w1_ref, w2_ref):
    rows, hidden = w1_ref.shape
    width = w2_ref.shape[1]
    parts = hidden // width
    for j in range(parts):
        block = g_ref[:, 2 * j * width : (2 * j + 1) * width].astype(F32)
        for i in range(n):
            at = (i * parts + j) * rows
            w1_ref[:, at : at + rows] = block[:, i * rows : (i + 1) * rows]
        w2_ref[j * rows : (j + 1) * rows] = g_ref[:, (2 * j + 1) * width : (2 * j + 2) * width].astype(F32)


def run_feed_out(g, n):
    rows = g.shape[0]
    width = rows * n
    parts = g.shape[1] // (2 * width)
    outs = (shape_of(rows, parts * width, dtype=F32), shape_of(parts * rows, width, dtype=F32))
    return pl.pallas_call(
        functools.partial(feed_out, n), out_shape=outs, cost_estimate=cost(3), compiler_params=params()
    )(g)


def tile_grad(a_ref, b_ref, out_ref):
    out_ref[...] = dot_tn(a_ref[...], b_ref[...]).astype(BF)


def run_tile_grad(a, b, after=()):
    a, b = flat(a), flat(b)
    rows, width = a.shape
    return launch(
        tile_grad, 6, (a, b), [pl.BlockSpec((rows, width // 2), lambda i: (0, i)), whole(b.shape)],
        pl.BlockSpec((width // 2, b.shape[1]), lambda i: (i, 0)), shape_of(width, b.shape[1]), (2,), after=after,
    )


def run_temporal_back_project(d_time, ol, chunk=2, after=()):
    frames, padded, width = d_time.shape
    block = frame_block(chunk, padded, width)
    dims = d_time.shape
    return launch(
        temporal_back_project, 8, (d_time, ol), [block, whole(ol.shape)], [block, block, whole((8, width))],
        (shape_of(*dims), shape_of(*dims), shape_of(8, width, dtype=F32)), (frames // chunk,), after=after,
    )


def run_temporal_back_attend(joined, d_mixed, after=()):
    frames, padded, width = d_mixed.shape
    wide = place_block(frames, 3 * width)
    return launch(
        temporal_back_attend, 20, (joined, d_mixed), [wide, place_block(frames, width)], wide,
        shape_of(frames, padded, 3 * width), (padded // TILE,), after=after,
    )


def run_temporal_back_finish(places, chunk, me, d_at, x, d_joined, qk, v_in, v, vecs, after=()):
    frames, padded, width = x.shape
    skip = len(after)

    def body(*refs):
        temporal_back_finish(places, *refs[:10], *refs[10 + skip :])

    def mixed_block(height, wide):
        return pl.BlockSpec((chunk, height, wide), lambda i, me: (jnp.bitwise_xor(i, me[0]), 0, 0))

    consts = (qk, v_in, v) + tuple(vecs)
    return pl.pallas_call(
        body,
        grid_spec=pltpu.PrefetchScalarGridSpec(
            num_scalar_prefetch=1,
            grid=(frames // chunk,),
            in_specs=[mixed_block(padded, width), mixed_block(padded, width), mixed_block(padded, 3 * width)]
            + wholes(consts) + [ANYWHERE] * skip,
            out_specs=[pl.BlockSpec((chunk, places, width), lambda i, me: (i, 0, 0)), whole((width, PAIR))],
            scratch_shapes=[pltpu.VMEM((PAIR, width), F32)],
        ),
        out_shape=(shape_of(frames, places, width), shape_of(width, PAIR)),
        cost_estimate=cost(13),
        compiler_params=params(),
    )(me, d_at, x, d_joined, *consts, *after)


AXES = ("dp_hi", "dp_lo", "seq_hi", "seq_lo")
SEQ = AXES[2:]


def swap(values, bit, n):
    return lax.ppermute(values, AXES, [(i, i ^ (1 << bit)) for i in range(n)])


class Gather:
    def __init__(self, values, n, order):
        self.n, self.bits, self.order = n, n.bit_length() - 1, list(order)
        self.me = lax.axis_index(AXES)
        self.tail = values.shape[1:]
        self.held = values.reshape((1,) * self.bits + values.shape)

    def start(self):
        self.bit = self.order.pop(0)
        self.got = swap(self.held, self.bit, self.n)
        return self.held

    def end(self, *after):
        got = gate(self.got, *after) if after else self.got
        axis = self.bits - 1 - self.bit
        high = ((self.me >> self.bit) & 1) == 1
        held = self.held
        self.held = jnp.where(high, jnp.concatenate([got, held], axis), jnp.concatenate([held, got], axis))

    def steps(self, count):
        for _ in range(count):
            self.start()
            self.end()

    def rest(self):
        self.steps(len(self.order))
        return self.result()

    def result(self):
        return self.held.reshape((-1,) + self.tail)


class Scatter:
    def __init__(self, values, n, order, axes):
        self.n, self.bits, self.order, self.axes = n, n.bit_length() - 1, list(order), axes
        self.rows, self.tail = values.shape[0] // n, values.shape[1:]
        self.me = lax.axis_index(AXES)
        self.held = values.reshape((2,) * self.bits + (self.rows,) + self.tail)

    def start(self):
        self.last = not self.order
        if self.last and self.axes:
            held = self.held.reshape((-1, self.rows) + self.tail)
            self.got = lax.all_to_all(held, self.axes, split_axis=0, concat_axis=0, tiled=True)
            return held
        bit = self.order.pop(0)
        axis = self.bits - 1 - bit
        mine = (self.me >> bit) & 1
        send = lax.dynamic_index_in_dim(self.held, 1 - mine, axis, keepdims=True)
        self.keep = lax.dynamic_index_in_dim(self.held, mine, axis, keepdims=True)
        self.got = swap(send, bit, self.n)
        return send

    def end(self, *after):
        got = gate(self.got, *after) if after else self.got
        if self.last:
            self.held = jnp.sum(got.astype(F32), axis=0)
        else:
            self.held = (self.keep.astype(F32) + got.astype(F32)).astype(self.held.dtype)

    def rest(self, *after):
        while self.order:
            self.start()
            self.end()
        if self.axes:
            self.start()
            self.end(*after)
        return self.held.astype(F32).reshape((self.rows,) + self.tail)


def on_device(n, tokens, tg, tb, t_in, t_out, t_lin, sg, sb, s_in, s_out, fg, fb, w1, b1, w2, cotangent):
    bits = n.bit_length() - 1
    top = tuple(range(bits - 1, 2, -1))
    order_a, order_b, order_c = top + (1, 2, 0), top + (2, 1, 0), (2,) + top + (1, 0)
    with_y, with_x = ((0, 2), (AXES[0], AXES[2])), ((0, 1), AXES[:2])
    rows, width = t_in.shape[0], t_in.shape[0] * n
    parts = w2.shape[0] // rows
    hidden = w1.shape[1]
    places = tokens.shape[2]
    frames = tokens.shape[0] * tokens.shape[1]
    extra = -places % TILE

    vecs = jnp.concatenate([tg[None], tb, sg[None], sb, fg[None], fb, b1.reshape(parts, rows)], axis=0)
    n_vec = vecs.shape[0]
    vec_cols = jnp.pad(vecs.T, ((0, 0), (0, 2 * HEAD_DIM - n_vec)))
    feed = jnp.concatenate(
        [
            w1.reshape(rows, n, parts, rows).transpose(0, 2, 1, 3).reshape(rows, hidden),
            w2.reshape(parts, rows, width).transpose(1, 0, 2).reshape(rows, hidden),
            s_in,
            s_out,
        ],
        axis=1,
    )
    feed = lax.all_gather(feed, AXES, axis=0, tiled=True)

    def own_clip(grid):
        clip = lax.all_to_all(grid, SEQ, split_axis=0, concat_axis=0, tiled=True)
        return jnp.pad(clip.reshape(frames, places, width), ((0, 0), (0, extra), (0, 0)))

    def own_frames(clip):
        return lax.all_to_all(clip.reshape(tokens.shape), SEQ, split_axis=0, concat_axis=0, tiled=True)

    def swap_pieces(clip, count):
        pieces = clip.reshape((count, tokens.shape[1]) + tokens.shape[2:])
        return [pieces[0]] + [lax.ppermute(pieces[k], AXES, [(i, i ^ k) for i in range(n)]) for k in range(1, count)]

    def in_order(got, me):
        step = 1
        while step < len(got):
            flip = (me & step) != 0
            got = [jnp.where(flip, got[j ^ step], got[j]) for j in range(len(got))]
            step *= 2
        return jnp.stack(got)

    x = own_clip(tokens)
    t_qk = Gather(t_in[:, : 2 * width], n, order_a)
    t_v = Gather(jnp.concatenate([t_in[:, 2 * width :], vec_cols], axis=1), n, order_c)
    t_ol = Gather(jnp.concatenate([t_out, t_lin], axis=1), n, order_b)
    t_qk_w, t_v_w = t_qk.rest(), t_v.rest()
    t_ol.steps(bits - 1)
    vec = t_v_w[:, width:].T[:16].astype(F32)
    norm_t, joined_t = run_temporal_project(x, t_qk_w, t_v_w, vec, after=(t_ol.start(),))
    t_ol.end(norm_t)
    t_ol_w = t_ol.result()
    mixed_t = run_temporal_attend(joined_t)
    proj_t, after_time = run_temporal_finish(x, mixed_t, t_ol_w, vec)
    cot = own_clip(gate(cotangent, norm_t))
    norm_s, joined_s, mixed_s, after_space = run_spatial_forward(places, after_time, feed, vec)
    out, d_after_space, norm_m, active, d_hidden, vec_f = run_feed(places, after_space, cot, feed, vec)
    output = own_frames(out)
    g_feed_all = run_feed_grads(norm_m, d_hidden, active, cot)
    g_feed = lax.psum_scatter(g_feed_all, AXES, scatter_dimension=0, tiled=True)
    o_w1, o_w2 = run_feed_out(g_feed, n)
    d_space, d_joined_s, d_after_time, d_time, vec_s = run_spatial_back(
        places, d_after_space, after_time, joined_s, feed, vec, after=(g_feed_all,)
    )
    g_space = run_join_grads(norm_s, d_joined_s, mixed_s, d_space, after=(output[0, :1, 0, :128],))

    def beside(chains, kernel, *args, after=()):
        sends = tuple(chain.start() for chain in chains)
        done = kernel(*args, after=sends + tuple(after))
        for chain in chains:
            chain.end(done[0] if isinstance(done, (tuple, list)) else done)
        return done

    gs = Scatter(g_space, n, *with_y)
    g_lin = beside((gs,), run_tile_grad, proj_t, d_time)
    sends = (gs.start(),)
    d_proj, d_mixed_t, vec_t1 = run_temporal_back_project(d_time, t_ol_w, after=sends)
    g_out = run_tile_grad(mixed_t, d_proj, after=sends)
    go = Scatter(jnp.concatenate([g_out, g_lin], axis=1), n, (0, 1, 2) + top[::-1], None)
    d_joined_t = beside((go,), run_temporal_back_attend, joined_t, d_mixed_t)
    gs.end(d_joined_t)
    sends = (gs.start(),)
    g_qkv = beside((go,), run_join_grads, norm_t, d_joined_t)
    half = 3 * width // 2
    gq = Scatter(g_qkv[:, :half], n, (0,), (AXES[0], AXES[1], AXES[2]))
    gq.start()
    me_seq = (lax.axis_index(SEQ)).astype(jnp.int32)
    g_x, vec_cols = beside(
        (go,), run_temporal_back_finish, places, tokens.shape[1], me_seq.reshape(1), d_after_time, x, d_joined_t,
        t_qk_w, t_v_w, vec, (vec_t1, vec_s, vec_f),
    )
    gs.end(g_x)
    gq.end(g_x, o_w1)
    gr = Scatter(jnp.concatenate([g_qkv[:, half:], gate(vec_cols, gq.held)], axis=1), n, *with_y)
    pieces = swap_pieces(g_x, tokens.shape[0])
    for after in ((), pieces[1:]):
        gr.start()
        gr.end(*after)
    g_q = gq.rest()
    g_x = in_order(pieces, me_seq)
    g_o = go.rest()
    g_r = gr.rest()
    g_s = gs.held.reshape(rows, 4 * width)
    g_i = jnp.concatenate([g_q, g_r[:, :half]], axis=1)
    v = g_r[:, half : half + n_vec].T
    return (
        output, g_x, v[0], v[1:4], g_i, g_o[:, :width], g_o[:, width : 2 * width],
        v[4], v[5:7], g_s[:, : 3 * width], g_s[:, 3 * width :], v[7], v[8:10],
        o_w1, v[10 : 10 + parts].reshape(-1), o_w2,
    )


def solution(mesh):
    dp, seq = AXES[:2], AXES[2:]
    dims = mesh.devices.shape
    halved = jax.sharding.Mesh(mesh.devices.reshape(dims[0] // 2, 2, dims[1] // 2, 2), AXES)
    shard = P(AXES)
    cols = P(None, AXES)
    mat = P(AXES, None)
    tok = P(dp, seq, None, None)
    in_specs = (tok, shard, cols, mat, mat, mat, shard, cols, mat, mat, shard, cols, mat, shard, mat, tok)
    out_specs = (tok, tok, shard, cols, mat, mat, mat, shard, cols, mat, mat, shard, cols, mat, shard, mat)
    return jax.shard_map(
        functools.partial(on_device, mesh.size), mesh=halved, in_specs=in_specs, out_specs=out_specs, check_vma=False
    )
```

```python
import functools

import jax
import jax.numpy as jnp
from jax import lax
from jax.experimental import pallas as pl
from jax.experimental.pallas import tpu as pltpu
from jax.sharding import PartitionSpec as P

HEADS = 12
HEAD_DIM = 64
PAIR = 2 * HEAD_DIM
PAIRS = HEADS // 2
TILE = 16
GROUP_T = 6
GROUP_S = 6
GROUP_SB = 3
GROUP_TB = 3
LOW = -1e30
BF = jnp.bfloat16
F32 = jnp.float32


def dot_nn(a, b):
    return lax.dot_general(a, b, (((1,), (0,)), ((), ())), preferred_element_type=F32)


def dot_nt(a, b):
    return lax.dot_general(a, b, (((1,), (1,)), ((), ())), preferred_element_type=F32)


def dot_tn(a, b):
    return lax.dot_general(a, b, (((0,), (0,)), ((), ())), preferred_element_type=F32)


def normalize(values):
    center = values - jnp.mean(values, axis=-1, keepdims=True)
    scale = lax.rsqrt(jnp.mean(center * center, axis=-1, keepdims=True) + 1e-05)
    return center * scale, scale


def norm_back(unit, scale, gain, grad):
    graded = grad * gain
    shift = jnp.mean(graded, axis=-1, keepdims=True)
    slope = jnp.mean(graded * unit, axis=-1, keepdims=True)
    return scale * (graded - shift - unit * slope)


def rows_of(block):
    return block.reshape(block.shape[0] * block.shape[1], block.shape[2])


def col_sum(values):
    return jnp.sum(values, axis=0, keepdims=True)


def lane_halves(shape):
    return lax.broadcasted_iota(jnp.int32, shape, len(shape) - 1) < HEAD_DIM


def half_masks():
    low_half = lane_halves((1, PAIR))
    return (
        jnp.where(low_half, 1.0, 0.0).astype(BF),
        jnp.where(low_half, 0.0, 1.0).astype(BF),
    )


def heads_forward(tiles, bias):
    low_mask, high_mask = half_masks()
    scale = HEAD_DIM ** (-0.5)
    scores = []
    for query, key, value in tiles:
        for mask in (low_mask, high_mask):
            scores.append(dot_nt(query * (mask * scale), key) + bias)
    tops = [jnp.max(s, axis=-1, keepdims=True) for s in scores]
    shares = [jnp.exp(s - top).astype(BF) for s, top in zip(scores, tops)]
    outs = []
    for at, share in enumerate(shares):
        value = tiles[at // 2][2]
        outs.append(dot_nn(share, jnp.concatenate([value, jnp.ones_like(value)], axis=1)))
    mixed = []
    for at in range(len(tiles)):
        first, second = outs[2 * at], outs[2 * at + 1]
        low_half = lane_halves((first.shape[0], PAIR))
        top = jnp.where(low_half, first[:, :PAIR], second[:, :PAIR])
        total = jnp.where(low_half, first[:, PAIR:], second[:, PAIR:])
        mixed.append((top / total).astype(BF))
    return mixed


def heads_backward(tiles, bias):
    low_mask, high_mask = half_masks()
    scale = HEAD_DIM ** (-0.5)
    turned = [key.T for query, key, value, grad in tiles]
    queries, grads, scores, grad_shares = [], [], [], []
    for query, key, value, grad in tiles:
        for mask in (low_mask, high_mask):
            queries.append(query * (mask * scale))
            grads.append(grad * mask)
            scores.append(dot_nt(key, queries[-1]) + bias)
            grad_shares.append(dot_nt(value, grads[-1]))
    tops = [jnp.max(s, axis=0, keepdims=True) for s in scores]
    raw = [jnp.exp(s - top) for s, top in zip(scores, tops)]
    inverse = [1.0 / jnp.sum(e, axis=0, keepdims=True) for e in raw]
    shares = [e * i for e, i in zip(raw, inverse)]
    terms = [jnp.sum(g * p, axis=0, keepdims=True) for g, p in zip(grad_shares, shares)]
    grad_scores = [(p * (g - t)).astype(BF) for p, g, t in zip(shares, grad_shares, terms)]
    shares = [p.astype(BF) for p in shares]
    out = []
    for at in range(len(tiles)):
        a, b = 2 * at, 2 * at + 1
        grad_value = dot_nn(shares[a], grads[a]) + dot_nn(shares[b], grads[b])
        grad_key = dot_nn(grad_scores[a], queries[a]) + dot_nn(grad_scores[b], queries[b])
        key_turned = turned[at]
        grad_query = jnp.concatenate(
            [dot_nn(key_turned[:HEAD_DIM], grad_scores[a]), dot_nn(key_turned[HEAD_DIM:], grad_scores[b])], axis=0
        )
        out.append(((grad_query * scale).astype(BF).T, grad_key.astype(BF), grad_value.astype(BF)))
    return out


def place_mask(size):
    row = lax.broadcasted_iota(jnp.int32, (size, size), 0)
    col = lax.broadcasted_iota(jnp.int32, (size, size), 1)
    return jnp.where(((row ^ col) & (TILE - 1)) == 0, 0.0, LOW)


def pair_cols(part, pair, width):
    start = part * width + pair * PAIR
    return slice(start, start + PAIR)


def temporal_project(x_ref, qk_ref, v_in_ref, v_ref, norm_ref, joined_ref):
    chunk, padded, width = x_ref.shape
    unit, scale = normalize(rows_of(x_ref[...]).astype(F32))
    norm = (unit * v_ref[0:1] + v_ref[1:2]).astype(BF)
    norm_ref[...] = norm.reshape(chunk, padded, width)
    for part in range(3):
        cols = slice(part * width, (part + 1) * width)
        weight = qk_ref[:, cols] if part < 2 else v_in_ref[:, :width]
        joined_ref[:, :, cols] = dot_nn(norm, weight).astype(BF).reshape(chunk, padded, width)


def temporal_attend(joined_ref, mixed_ref):
    frames, tile, width = mixed_ref.shape
    bias = place_mask(frames * tile)
    for first in range(0, PAIRS, GROUP_T):
        group = range(first, first + GROUP_T)
        tiles = [[rows_of(joined_ref[:, :, pair_cols(i, pair, width)]) for i in range(3)] for pair in group]
        for pair, mixed in zip(group, heads_forward(tiles, bias)):
            mixed_ref[:, :, pair_cols(0, pair, width)] = mixed.reshape(frames, tile, PAIR)


def temporal_finish(x_ref, mixed_ref, ol_ref, v_ref, proj_ref, after_ref):
    chunk, padded, width = x_ref.shape
    proj = (dot_nn(rows_of(mixed_ref[...]), ol_ref[:, :width]) + v_ref[2:3]).astype(BF)
    proj_ref[...] = proj.reshape(chunk, padded, width)
    branch = (dot_nn(proj, ol_ref[:, width:]) + v_ref[3:4]).astype(BF)
    after = rows_of(x_ref[...]).astype(F32) + branch.astype(F32)
    after_ref[...] = after.reshape(chunk, padded, width)


def spatial_forward(places, after_ref, s_ref, v_ref, norm_ref, joined_ref, mixed_ref, space_ref):
    chunk, padded, width = after_ref.shape
    after = rows_of(after_ref[...])
    unit, scale = normalize(after)
    norm = (unit * v_ref[4:5] + v_ref[5:6]).astype(BF)
    norm_ref[...] = norm.reshape(chunk, padded, width)
    for part in range(3):
        cols = slice(part * width, (part + 1) * width)
        joined_ref[:, :, cols] = dot_nn(norm, s_ref[:, cols]).astype(BF).reshape(chunk, padded, width)
    allowed = jnp.where(lax.broadcasted_iota(jnp.int32, (1, padded), 1) < places, 0.0, LOW)
    for frame in range(chunk):
        for first in range(0, PAIRS, GROUP_S):
            group = range(first, first + GROUP_S)
            tiles = [[joined_ref[frame, :, pair_cols(i, pair, width)] for i in range(3)] for pair in group]
            for pair, mixed in zip(group, heads_forward(tiles, allowed)):
                mixed_ref[frame, :, pair_cols(0, pair, width)] = mixed
    space = after + dot_nn(rows_of(mixed_ref[...]), s_ref[:, 3 * width :]) + v_ref[6:7]
    space_ref[...] = space.reshape(chunk, padded, width)


def gelu_parts(hidden):
    phi = 0.5 * (1.0 + lax.erf(hidden * 0.7071067811865476))
    density = jnp.exp(-0.5 * hidden * hidden) * 0.3989422804014327
    return phi, density


def feed_both(places, space_ref, cot_ref, w1_ref, w2_ref, v_ref, out_ref, grad_ref, norm_ref, active_ref, dhid_ref, vec_ref):
    chunk, padded, width = space_ref.shape
    blocks = w1_ref.shape[1] // width

    @pl.when(pl.program_id(0) == 0)
    def _():
        vec_ref[...] = jnp.zeros_like(vec_ref)

    space = rows_of(space_ref[...])
    cot = rows_of(cot_ref[...])
    unit, scale = normalize(space)
    norm = (unit * v_ref[7:8] + v_ref[8:9]).astype(BF)
    norm_ref[...] = norm.reshape(chunk, padded, width)
    out = space + v_ref[9:10]
    d_norm = jnp.zeros_like(space)
    for block in range(blocks):
        cols = slice(block * width, (block + 1) * width)
        hidden = dot_nn(norm, w1_ref[:, cols]) + v_ref[10 + block : 11 + block]
        phi, density = gelu_parts(hidden)
        active = (hidden * phi).astype(BF)
        active_ref[:, :, cols] = active.reshape(chunk, padded, width)
        out += dot_nn(active, w2_ref[:, cols])
        d_hidden = dot_nt(cot, w2_ref[:, cols]) * (phi + hidden * density)
        vec_ref[3 + block : 4 + block] += col_sum(d_hidden.astype(BF).astype(F32))
        d_hidden = d_hidden.astype(BF)
        dhid_ref[:, :, cols] = d_hidden.reshape(chunk, padded, width)
        d_norm += dot_nt(d_hidden, w1_ref[:, cols])
    for frame in range(chunk):
        out_ref[frame] = out[frame * padded : frame * padded + places].astype(BF)
    vec_ref[0:1] += col_sum(d_norm * unit)
    vec_ref[1:2] += col_sum(d_norm)
    vec_ref[2:3] += col_sum(cot.astype(F32))
    grad = cot.astype(F32) + norm_back(unit, scale, v_ref[7:8], d_norm)
    grad_ref[...] = grad.reshape(chunk, padded, width)


def feed_grads(norm_ref, dhid_ref, active_ref, cot_ref, out_ref, norm_turned, cot_turned):
    width = norm_ref.shape[1]

    @pl.when(pl.program_id(0) == 0)
    def _():
        norm_turned[...] = norm_ref[...].T
        cot_turned[...] = cot_ref[...].T

    out_ref[:, :width] = dot_nn(norm_turned[...], dhid_ref[...]).astype(BF)
    out_ref[:, width:] = dot_nn(cot_turned[...], active_ref[...]).astype(BF).T


def spatial_back(places, grad_ref, after_ref, joined_ref, s_ref, v_ref, dspace_ref, djoin_ref, dat_ref, dtime_ref, vec_ref, dmix_ref):
    chunk, padded, width = grad_ref.shape

    @pl.when(pl.program_id(0) == 0)
    def _():
        vec_ref[...] = jnp.zeros_like(vec_ref)

    grad = rows_of(grad_ref[...])
    d_space = grad.astype(BF)
    dspace_ref[...] = d_space.reshape(chunk, padded, width)
    vec_ref[2:3] += col_sum(d_space.astype(F32))
    dmix_ref[...] = dot_nt(d_space, s_ref[:, 3 * width :]).astype(BF).reshape(chunk, padded, width)
    allowed = jnp.where(lax.broadcasted_iota(jnp.int32, (padded, 1), 0) < places, 0.0, LOW)
    for frame in range(chunk):
        for first in range(0, PAIRS, GROUP_SB):
            group = range(first, first + GROUP_SB)
            tiles = [
                [joined_ref[frame, :, pair_cols(i, pair, width)] for i in range(3)]
                + [dmix_ref[frame, :, pair_cols(0, pair, width)]]
                for pair in group
            ]
            for pair, grads in zip(group, heads_backward(tiles, allowed)):
                for i in range(3):
                    djoin_ref[frame, :, pair_cols(i, pair, width)] = grads[i]
    d_joined = rows_of(djoin_ref[...])
    d_norm = dot_nt(d_joined, s_ref[:, : 3 * width])
    unit, scale = normalize(rows_of(after_ref[...]))
    vec_ref[0:1] += col_sum(d_norm * unit)
    vec_ref[1:2] += col_sum(d_norm)
    d_time = grad + norm_back(unit, scale, v_ref[4:5], d_norm)
    dat_ref[...] = d_time.reshape(chunk, padded, width)
    dtime_ref[...] = d_time.astype(BF).reshape(chunk, padded, width)


def turned_grads(count, norm_ref, djoin_ref, *refs):
    i = pl.program_id(0)
    out_ref, norm_turned = refs[-2:]

    @pl.when(i == 0)
    def _():
        norm_turned[...] = norm_ref[...].T

    @pl.when(i < count)
    def _():
        out_ref[...] = dot_nn(norm_turned[...], djoin_ref[...]).astype(BF)

    if len(refs) > 2:

        @pl.when(i == count)
        def _():
            out_ref[...] = dot_tn(refs[0][...], refs[1][...]).astype(BF)


def temporal_back_project(dtime_ref, ol_ref, dproj_ref, dmix_ref, vec_ref):
    chunk, padded, width = dtime_ref.shape

    @pl.when(pl.program_id(0) == 0)
    def _():
        vec_ref[...] = jnp.zeros_like(vec_ref)

    d_time = rows_of(dtime_ref[...])
    vec_ref[1:2] += col_sum(d_time.astype(F32))
    d_proj = dot_nt(d_time, ol_ref[:, width:]).astype(BF)
    vec_ref[0:1] += col_sum(d_proj.astype(F32))
    dproj_ref[...] = d_proj.reshape(chunk, padded, width)
    dmix_ref[...] = dot_nt(d_proj, ol_ref[:, :width]).astype(BF).reshape(chunk, padded, width)


def temporal_back_attend(joined_ref, dmix_ref, djoin_ref):
    frames, tile, width = dmix_ref.shape
    bias = place_mask(frames * tile)
    for first in range(0, PAIRS, GROUP_TB):
        group = range(first, first + GROUP_TB)
        tiles = [
            [rows_of(joined_ref[:, :, pair_cols(i, pair, width)]) for i in range(3)]
            + [rows_of(dmix_ref[:, :, pair_cols(0, pair, width)])]
            for pair in group
        ]
        for pair, grads in zip(group, heads_backward(tiles, bias)):
            for i in range(3):
                djoin_ref[:, :, pair_cols(i, pair, width)] = grads[i].reshape(frames, tile, PAIR)


def temporal_back_finish(
    places, me_ref, dat_ref, x_ref, djoin_ref, qk_ref, v_in_ref, v_ref, vec_t_ref, vec_s_ref, vec_f_ref,
    gx_ref, turned_ref, vec_ref,
):
    chunk, padded, width = x_ref.shape

    @pl.when(pl.program_id(0) == 0)
    def _():
        vec_ref[...] = jnp.zeros_like(vec_ref)
        vec_ref[2:4] = vec_t_ref[0:2]
        vec_ref[4:7] = vec_s_ref[0:3]
        vec_ref[7:14] = vec_f_ref[0:7]

    d_joined = rows_of(djoin_ref[...])
    d_norm = dot_nt(d_joined[:, : 2 * width], qk_ref[...]) + dot_nt(d_joined[:, 2 * width :], v_in_ref[:, :width])
    d_norm = d_norm.astype(BF).astype(F32)
    unit, scale = normalize(rows_of(x_ref[...]).astype(F32))
    vec_ref[0:1] += col_sum(d_norm * unit)
    vec_ref[1:2] += col_sum(d_norm)
    grad = rows_of(dat_ref[...]) + norm_back(unit, scale, v_ref[0:1], d_norm)
    gx_ref[...] = grad.astype(BF).reshape(chunk, padded, width)[:, :places]

    @pl.when(pl.program_id(0) == pl.num_programs(0) - 1)
    def _():
        turned_ref[...] = vec_ref[...].T.astype(BF)


def whole(shape):
    return pl.BlockSpec(shape, lambda *i: (0,) * len(shape))


def cost(micros):
    return pl.CostEstimate(flops=int(micros * 1e8), bytes_accessed=0, transcendentals=0)


def params(mib=60):
    return pltpu.CompilerParams(vmem_limit_bytes=mib << 20)


def shape_of(*dims, dtype=BF):
    return jax.ShapeDtypeStruct(dims, dtype)


ANYWHERE = pl.BlockSpec(memory_space=pl.ANY)


def launch(kernel, micros, args, in_specs, out_specs, out_shape, grid, scratch=(), after=()):
    count, skip = len(args), len(after)

    def body(*refs):
        kernel(*refs[:count], *refs[count + skip :])

    return pl.pallas_call(
        body,
        grid=grid,
        in_specs=list(in_specs) + [ANYWHERE] * skip,
        out_specs=out_specs,
        out_shape=out_shape,
        scratch_shapes=list(scratch),
        cost_estimate=cost(micros),
        compiler_params=params(),
    )(*args, *after)


def gate(value, *after):
    return lax.optimization_barrier((value,) + after)[0]


def frame_block(chunk, padded, width):
    return pl.BlockSpec((chunk, padded, width), lambda i: (i, 0, 0))


def place_block(frames, width):
    return pl.BlockSpec((frames, TILE, width), lambda i: (0, i, 0))


def wholes(arrays):
    return [whole(a.shape) for a in arrays]


def flat(a):
    return a.reshape(-1, a.shape[-1])


def run_temporal_project(x, qk, v_in, v, chunk=2, after=()):
    frames, padded, width = x.shape
    block, wide = frame_block(chunk, padded, width), frame_block(chunk, padded, 3 * width)
    return launch(
        temporal_project, 9, (x, qk, v_in, v), [block] + wholes((qk, v_in, v)), [block, wide],
        (shape_of(*x.shape), shape_of(frames, padded, 3 * width)), (frames // chunk,), after=after,
    )


def run_temporal_attend(joined, after=()):
    frames, padded, wide = joined.shape
    width = wide // 3
    return launch(
        temporal_attend, 14, (joined,), [place_block(frames, wide)], place_block(frames, width),
        shape_of(frames, padded, width), (padded // TILE,), after=after,
    )


def run_temporal_finish(x, mixed, ol, v, chunk=2, after=()):
    frames, padded, width = x.shape
    block = frame_block(chunk, padded, width)
    return launch(
        temporal_finish, 8, (x, mixed, ol, v), [block, block] + wholes((ol, v)), [block, block],
        (shape_of(*x.shape), shape_of(*x.shape, dtype=F32)), (frames // chunk,), after=after,
    )


def run_spatial_forward(places, attended, pack, v, chunk=2, after=()):
    frames, padded, width = attended.shape
    block, wide = frame_block(chunk, padded, width), frame_block(chunk, padded, 3 * width)
    dims = attended.shape
    return launch(
        functools.partial(spatial_forward, places), 23, (attended, pack, v),
        [block, pl.BlockSpec((width, 4 * width), lambda i: (0, 2)), whole(v.shape)],
        [block, wide, block, block],
        (shape_of(*dims), shape_of(frames, padded, 3 * width), shape_of(*dims), shape_of(*dims, dtype=F32)),
        (frames // chunk,), after=after,
    )


def run_feed(places, space, cot, pack, v, chunk=2, after=()):
    frames, padded, width = space.shape
    hidden = 4 * width
    block, wide = frame_block(chunk, padded, width), frame_block(chunk, padded, hidden)
    dims = space.shape
    return launch(
        functools.partial(feed_both, places), 45, (space, cot, pack, pack, v),
        [
            block, block,
            pl.BlockSpec((width, hidden), lambda i: (0, 0)),
            pl.BlockSpec((width, hidden), lambda i: (0, 1)),
            whole(v.shape),
        ],
        [frame_block(chunk, places, width), block, block, wide, wide, whole((8, width))],
        (
            shape_of(frames, places, width), shape_of(*dims, dtype=F32), shape_of(*dims),
            shape_of(frames, padded, hidden), shape_of(frames, padded, hidden), shape_of(8, width, dtype=F32),
        ),
        (frames // chunk,), after=after,
    )


def run_feed_grads(norm, d_hidden, active, cot, after=()):
    norm, d_hidden, active, cot = flat(norm), flat(d_hidden), flat(active), flat(cot)
    rows, width = norm.shape
    blocks = d_hidden.shape[1] // width
    part = pl.BlockSpec((rows, width), lambda i: (0, i))
    return launch(
        feed_grads, 25, (norm, d_hidden, active, cot), [whole((rows, width)), part, part, whole((rows, width))],
        pl.BlockSpec((width, 2 * width), lambda i: (0, i)), shape_of(width, 2 * width * blocks), (blocks,),
        scratch=[pltpu.VMEM((width, rows), BF), pltpu.VMEM((width, rows), BF)], after=after,
    )


def run_spatial_back(places, grad, attended, joined, pack, v, chunk=2, after=()):
    frames, padded, width = grad.shape
    block, wide = frame_block(chunk, padded, width), frame_block(chunk, padded, 3 * width)
    dims = grad.shape
    return launch(
        functools.partial(spatial_back, places), 42, (grad, attended, joined, pack, v),
        [block, block, wide, pl.BlockSpec((width, 4 * width), lambda i: (0, 2)), whole(v.shape)],
        [block, wide, block, block, whole((8, width))],
        (
            shape_of(*dims), shape_of(frames, padded, 3 * width), shape_of(*dims, dtype=F32), shape_of(*dims),
            shape_of(8, width, dtype=F32),
        ),
        (frames // chunk,), scratch=[pltpu.VMEM((chunk, padded, width), BF)], after=after,
    )


def run_join_grads(norm, d_joined, *more, after=()):
    norm, d_joined = flat(norm), flat(d_joined)
    more = [flat(a) for a in more]
    rows, width = norm.shape
    count = d_joined.shape[1] // width
    steps = count + (1 if more else 0)
    return launch(
        functools.partial(turned_grads, count), 4 * steps, (norm, d_joined, *more),
        [whole((rows, width)), pl.BlockSpec((rows, width), lambda i: (0, jnp.minimum(i, count - 1)))] + wholes(more),
        pl.BlockSpec((width, width), lambda i: (0, i)), shape_of(width, steps * width), (steps,),
        scratch=[pltpu.VMEM((width, rows), BF)], after=after,
    )


def feed_out(n, g_ref, w1_ref, w2_ref):
    rows, hidden = w1_ref.shape
    width = w2_ref.shape[1]
    parts = hidden // width
    for j in range(parts):
        block = g_ref[:, 2 * j * width : (2 * j + 1) * width].astype(F32)
        for i in range(n):
            at = (i * parts + j) * rows
            w1_ref[:, at : at + rows] = block[:, i * rows : (i + 1) * rows]
        w2_ref[j * rows : (j + 1) * rows] = g_ref[:, (2 * j + 1) * width : (2 * j + 2) * width].astype(F32)


def run_feed_out(g, n):
    rows = g.shape[0]
    width = rows * n
    parts = g.shape[1] // (2 * width)
    outs = (shape_of(rows, parts * width, dtype=F32), shape_of(parts * rows, width, dtype=F32))
    return pl.pallas_call(
        functools.partial(feed_out, n), out_shape=outs, cost_estimate=cost(3), compiler_params=params()
    )(g)


def tile_grad(a_ref, b_ref, out_ref):
    out_ref[...] = dot_tn(a_ref[...], b_ref[...]).astype(BF)


def run_tile_grad(a, b, after=()):
    a, b = flat(a), flat(b)
    rows, width = a.shape
    return launch(
        tile_grad, 6, (a, b), [pl.BlockSpec((rows, width // 2), lambda i: (0, i)), whole(b.shape)],
        pl.BlockSpec((width // 2, b.shape[1]), lambda i: (i, 0)), shape_of(width, b.shape[1]), (2,), after=after,
    )


def run_temporal_back_project(d_time, ol, chunk=2, after=()):
    frames, padded, width = d_time.shape
    block = frame_block(chunk, padded, width)
    dims = d_time.shape
    return launch(
        temporal_back_project, 8, (d_time, ol), [block, whole(ol.shape)], [block, block, whole((8, width))],
        (shape_of(*dims), shape_of(*dims), shape_of(8, width, dtype=F32)), (frames // chunk,), after=after,
    )


def run_temporal_back_attend(joined, d_mixed, after=()):
    frames, padded, width = d_mixed.shape
    wide = place_block(frames, 3 * width)
    return launch(
        temporal_back_attend, 20, (joined, d_mixed), [wide, place_block(frames, width)], wide,
        shape_of(frames, padded, 3 * width), (padded // TILE,), after=after,
    )


def run_temporal_back_finish(places, chunk, me, d_at, x, d_joined, qk, v_in, v, vecs, after=()):
    frames, padded, width = x.shape
    skip = len(after)

    def body(*refs):
        temporal_back_finish(places, *refs[:10], *refs[10 + skip :])

    def mixed_block(height, wide):
        return pl.BlockSpec((chunk, height, wide), lambda i, me: (jnp.bitwise_xor(i, me[0]), 0, 0))

    consts = (qk, v_in, v) + tuple(vecs)
    return pl.pallas_call(
        body,
        grid_spec=pltpu.PrefetchScalarGridSpec(
            num_scalar_prefetch=1,
            grid=(frames // chunk,),
            in_specs=[mixed_block(padded, width), mixed_block(padded, width), mixed_block(padded, 3 * width)]
            + wholes(consts) + [ANYWHERE] * skip,
            out_specs=[pl.BlockSpec((chunk, places, width), lambda i, me: (i, 0, 0)), whole((width, PAIR))],
            scratch_shapes=[pltpu.VMEM((PAIR, width), F32)],
        ),
        out_shape=(shape_of(frames, places, width), shape_of(width, PAIR)),
        cost_estimate=cost(13),
        compiler_params=params(),
    )(me, d_at, x, d_joined, *consts, *after)


AXES = ("dp_hi", "dp_lo", "seq_hi", "seq_lo")
SEQ = AXES[2:]


def swap(values, bit, n):
    return lax.ppermute(values, AXES, [(i, i ^ (1 << bit)) for i in range(n)])


class Gather:
    def __init__(self, values, n, order):
        self.n, self.bits, self.order = n, n.bit_length() - 1, list(order)
        self.me = lax.axis_index(AXES)
        self.tail = values.shape[1:]
        self.held = values.reshape((1,) * self.bits + values.shape)

    def start(self):
        self.bit = self.order.pop(0)
        self.got = swap(self.held, self.bit, self.n)
        return self.held

    def end(self, *after):
        got = gate(self.got, *after) if after else self.got
        axis = self.bits - 1 - self.bit
        high = ((self.me >> self.bit) & 1) == 1
        held = self.held
        self.held = jnp.where(high, jnp.concatenate([got, held], axis), jnp.concatenate([held, got], axis))

    def steps(self, count):
        for _ in range(count):
            self.start()
            self.end()

    def rest(self):
        self.steps(len(self.order))
        return self.result()

    def result(self):
        return self.held.reshape((-1,) + self.tail)


class Scatter:
    def __init__(self, values, n, order, axes):
        self.n, self.bits, self.order, self.axes = n, n.bit_length() - 1, list(order), axes
        self.rows, self.tail = values.shape[0] // n, values.shape[1:]
        self.me = lax.axis_index(AXES)
        self.held = values.reshape((2,) * self.bits + (self.rows,) + self.tail)

    def start(self):
        self.last = not self.order
        if self.last and self.axes:
            held = self.held.reshape((-1, self.rows) + self.tail)
            self.got = lax.all_to_all(held, self.axes, split_axis=0, concat_axis=0, tiled=True)
            return held
        bit = self.order.pop(0)
        axis = self.bits - 1 - bit
        mine = (self.me >> bit) & 1
        send = lax.dynamic_index_in_dim(self.held, 1 - mine, axis, keepdims=True)
        self.keep = lax.dynamic_index_in_dim(self.held, mine, axis, keepdims=True)
        self.got = swap(send, bit, self.n)
        return send

    def end(self, *after):
        got = gate(self.got, *after) if after else self.got
        if self.last:
            self.held = jnp.sum(got.astype(F32), axis=0)
        else:
            self.held = (self.keep.astype(F32) + got.astype(F32)).astype(self.held.dtype)

    def rest(self, *after):
        while self.order:
            self.start()
            self.end()
        if self.axes:
            self.start()
            self.end(*after)
        return self.held.astype(F32).reshape((self.rows,) + self.tail)


def on_device(n, tokens, tg, tb, t_in, t_out, t_lin, sg, sb, s_in, s_out, fg, fb, w1, b1, w2, cotangent):
    bits = n.bit_length() - 1
    top = tuple(range(bits - 1, 2, -1))
    order_a, order_b, order_c = top + (1, 2, 0), top + (2, 1, 0), (2,) + top + (1, 0)
    with_y, with_x = ((0, 2), (AXES[0], AXES[2])), ((0, 1), AXES[:2])
    rows, width = t_in.shape[0], t_in.shape[0] * n
    parts = w2.shape[0] // rows
    hidden = w1.shape[1]
    places = tokens.shape[2]
    frames = tokens.shape[0] * tokens.shape[1]
    extra = -places % TILE

    vecs = jnp.concatenate([tg[None], tb, sg[None], sb, fg[None], fb, b1.reshape(parts, rows)], axis=0)
    n_vec = vecs.shape[0]
    vec_cols = jnp.pad(vecs.T, ((0, 0), (0, 2 * HEAD_DIM - n_vec)))
    feed = jnp.concatenate(
        [
            w1.reshape(rows, n, parts, rows).transpose(0, 2, 1, 3).reshape(rows, hidden),
            w2.reshape(parts, rows, width).transpose(1, 0, 2).reshape(rows, hidden),
            s_in,
            s_out,
        ],
        axis=1,
    )
    feed = lax.all_gather(feed, AXES, axis=0, tiled=True)

    def own_clip(grid):
        clip = lax.all_to_all(grid, SEQ, split_axis=0, concat_axis=0, tiled=True)
        return jnp.pad(clip.reshape(frames, places, width), ((0, 0), (0, extra), (0, 0)))

    def own_frames(clip):
        return lax.all_to_all(clip.reshape(tokens.shape), SEQ, split_axis=0, concat_axis=0, tiled=True)

    def swap_pieces(clip, count):
        pieces = clip.reshape((count, tokens.shape[1]) + tokens.shape[2:])
        return [pieces[0]] + [lax.ppermute(pieces[k], AXES, [(i, i ^ k) for i in range(n)]) for k in range(1, count)]

    def in_order(got, me):
        step = 1
        while step < len(got):
            flip = (me & step) != 0
            got = [jnp.where(flip, got[j ^ step], got[j]) for j in range(len(got))]
            step *= 2
        return jnp.stack(got)

    x = own_clip(tokens)
    t_qk = Gather(t_in[:, : 2 * width], n, order_a)
    t_v = Gather(jnp.concatenate([t_in[:, 2 * width :], vec_cols], axis=1), n, order_c)
    t_ol = Gather(jnp.concatenate([t_out, t_lin], axis=1), n, order_b)
    t_qk_w, t_v_w = t_qk.rest(), t_v.rest()
    t_ol.steps(bits - 1)
    vec = t_v_w[:, width:].T[:16].astype(F32)
    norm_t, joined_t = run_temporal_project(x, t_qk_w, t_v_w, vec, after=(t_ol.start(),))
    t_ol.end(norm_t)
    t_ol_w = t_ol.result()
    mixed_t = run_temporal_attend(joined_t)
    proj_t, after_time = run_temporal_finish(x, mixed_t, t_ol_w, vec)
    cot = own_clip(gate(cotangent, norm_t))
    norm_s, joined_s, mixed_s, after_space = run_spatial_forward(places, after_time, feed, vec)
    out, d_after_space, norm_m, active, d_hidden, vec_f = run_feed(places, after_space, cot, feed, vec)
    output = own_frames(out)
    g_feed_all = run_feed_grads(norm_m, d_hidden, active, cot)
    g_feed = lax.psum_scatter(g_feed_all, AXES, scatter_dimension=0, tiled=True)
    o_w1, o_w2 = run_feed_out(g_feed, n)
    d_space, d_joined_s, d_after_time, d_time, vec_s = run_spatial_back(
        places, d_after_space, after_time, joined_s, feed, vec, after=(g_feed_all,)
    )
    g_space = run_join_grads(norm_s, d_joined_s, mixed_s, d_space, after=(output[0, :1, 0, :128],))

    def beside(chains, kernel, *args, after=()):
        sends = tuple(chain.start() for chain in chains)
        done = kernel(*args, after=sends + tuple(after))
        for chain in chains:
            chain.end(done[0] if isinstance(done, (tuple, list)) else done)
        return done

    gs = Scatter(g_space, n, *with_y)
    g_lin = beside((gs,), run_tile_grad, proj_t, d_time)
    sends = (gs.start(),)
    d_proj, d_mixed_t, vec_t1 = run_temporal_back_project(d_time, t_ol_w, after=sends)
    g_out = run_tile_grad(mixed_t, d_proj, after=sends)
    go = Scatter(jnp.concatenate([g_out, g_lin], axis=1), n, (0, 1, 2) + top[::-1], None)
    d_joined_t = beside((go,), run_temporal_back_attend, joined_t, d_mixed_t)
    gs.end(d_joined_t)
    sends = (gs.start(),)
    g_qkv = beside((go,), run_join_grads, norm_t, d_joined_t)
    half = 3 * width // 2
    gq = Scatter(g_qkv[:, :half], n, (0,), (AXES[0], AXES[1], AXES[2]))
    gq.start()
    me_seq = (lax.axis_index(SEQ)).astype(jnp.int32)
    g_x, vec_cols = beside(
        (go,), run_temporal_back_finish, places, tokens.shape[1], me_seq.reshape(1), d_after_time, x, d_joined_t,
        t_qk_w, t_v_w, vec, (vec_t1, vec_s, vec_f),
    )
    gs.end(g_x)
    gq.end(g_x, o_w1)
    gr = Scatter(jnp.concatenate([g_qkv[:, half:], gate(vec_cols, gq.held)], axis=1), n, *with_y)
    pieces = swap_pieces(g_x, tokens.shape[0])
    for after in ((), pieces[1:]):
        gr.start()
        gr.end(*after)
    g_q = gq.rest()
    g_x = in_order(pieces, me_seq)
    g_o = go.rest()
    g_r = gr.rest()
    g_s = gs.held.reshape(rows, 4 * width)
    g_i = jnp.concatenate([g_q, g_r[:, :half]], axis=1)
    v = g_r[:, half : half + n_vec].T
    return (
        output, g_x, v[0], v[1:4], g_i, g_o[:, :width], g_o[:, width : 2 * width],
        v[4], v[5:7], g_s[:, : 3 * width], g_s[:, 3 * width :], v[7], v[8:10],
        o_w1, v[10 : 10 + parts].reshape(-1), o_w2,
    )


def solution(mesh):
    dp, seq = AXES[:2], AXES[2:]
    dims = mesh.devices.shape
    halved = jax.sharding.Mesh(mesh.devices.reshape(dims[0] // 2, 2, dims[1] // 2, 2), AXES)
    shard = P(AXES)
    cols = P(None, AXES)
    mat = P(AXES, None)
    tok = P(dp, seq, None, None)
    in_specs = (tok, shard, cols, mat, mat, mat, shard, cols, mat, mat, shard, cols, mat, shard, mat, tok)
    out_specs = (tok, tok, shard, cols, mat, mat, mat, shard, cols, mat, mat, shard, cols, mat, shard, mat)
    return jax.shard_map(
        functools.partial(on_device, mesh.size), mesh=halved, in_specs=in_specs, out_specs=out_specs, check_vma=False
    )
```

```python
import functools

import jax
import jax.numpy as jnp
from jax import lax
from jax.experimental import pallas as pl
from jax.experimental.pallas import tpu as pltpu
from jax.sharding import PartitionSpec as P

HEADS = 12
HEAD_DIM = 64
PAIR = 2 * HEAD_DIM
PAIRS = HEADS // 2
TILE = 16
GROUP_T = 6
GROUP_S = 6
GROUP_SB = 3
GROUP_TB = 3
LOW = -1e30
BF = jnp.bfloat16
F32 = jnp.float32


def dot_nn(a, b):
    return lax.dot_general(a, b, (((1,), (0,)), ((), ())), preferred_element_type=F32)


def dot_nt(a, b):
    return lax.dot_general(a, b, (((1,), (1,)), ((), ())), preferred_element_type=F32)


def dot_tn(a, b):
    return lax.dot_general(a, b, (((0,), (0,)), ((), ())), preferred_element_type=F32)


def normalize(values):
    center = values - jnp.mean(values, axis=-1, keepdims=True)
    scale = lax.rsqrt(jnp.mean(center * center, axis=-1, keepdims=True) + 1e-05)
    return center * scale, scale


def norm_back(unit, scale, gain, grad):
    graded = grad * gain
    shift = jnp.mean(graded, axis=-1, keepdims=True)
    slope = jnp.mean(graded * unit, axis=-1, keepdims=True)
    return scale * (graded - shift - unit * slope)


def rows_of(block):
    return block.reshape(block.shape[0] * block.shape[1], block.shape[2])


def col_sum(values):
    return jnp.sum(values, axis=0, keepdims=True)


def lane_halves(shape):
    return lax.broadcasted_iota(jnp.int32, shape, len(shape) - 1) < HEAD_DIM


def half_masks():
    low_half = lane_halves((1, PAIR))
    return (
        jnp.where(low_half, 1.0, 0.0).astype(BF),
        jnp.where(low_half, 0.0, 1.0).astype(BF),
    )


def heads_forward(tiles, bias):
    low_mask, high_mask = half_masks()
    scale = HEAD_DIM ** (-0.5)
    scores = []
    for query, key, value in tiles:
        for mask in (low_mask, high_mask):
            scores.append(dot_nt(query * (mask * scale), key) + bias)
    tops = [jnp.max(s, axis=-1, keepdims=True) for s in scores]
    shares = [jnp.exp(s - top).astype(BF) for s, top in zip(scores, tops)]
    outs = []
    for at, share in enumerate(shares):
        value = tiles[at // 2][2]
        outs.append(dot_nn(share, jnp.concatenate([value, jnp.ones_like(value)], axis=1)))
    mixed = []
    for at in range(len(tiles)):
        first, second = outs[2 * at], outs[2 * at + 1]
        low_half = lane_halves((first.shape[0], PAIR))
        top = jnp.where(low_half, first[:, :PAIR], second[:, :PAIR])
        total = jnp.where(low_half, first[:, PAIR:], second[:, PAIR:])
        mixed.append((top / total).astype(BF))
    return mixed


def heads_backward(tiles, bias):
    low_mask, high_mask = half_masks()
    scale = HEAD_DIM ** (-0.5)
    turned = [key.T for query, key, value, grad in tiles]
    queries, grads, scores, grad_shares = [], [], [], []
    for query, key, value, grad in tiles:
        for mask in (low_mask, high_mask):
            queries.append(query * (mask * scale))
            grads.append(grad * mask)
            scores.append(dot_nt(key, queries[-1]) + bias)
            grad_shares.append(dot_nt(value, grads[-1]))
    tops = [jnp.max(s, axis=0, keepdims=True) for s in scores]
    raw = [jnp.exp(s - top) for s, top in zip(scores, tops)]
    inverse = [1.0 / jnp.sum(e, axis=0, keepdims=True) for e in raw]
    shares = [e * i for e, i in zip(raw, inverse)]
    terms = [jnp.sum(g * p, axis=0, keepdims=True) for g, p in zip(grad_shares, shares)]
    grad_scores = [(p * (g - t)).astype(BF) for p, g, t in zip(shares, grad_shares, terms)]
    shares = [p.astype(BF) for p in shares]
    out = []
    for at in range(len(tiles)):
        a, b = 2 * at, 2 * at + 1
        grad_value = dot_nn(shares[a], grads[a]) + dot_nn(shares[b], grads[b])
        grad_key = dot_nn(grad_scores[a], queries[a]) + dot_nn(grad_scores[b], queries[b])
        key_turned = turned[at]
        grad_query = jnp.concatenate(
            [dot_nn(key_turned[:HEAD_DIM], grad_scores[a]), dot_nn(key_turned[HEAD_DIM:], grad_scores[b])], axis=0
        )
        out.append(((grad_query * scale).astype(BF).T, grad_key.astype(BF), grad_value.astype(BF)))
    return out


def place_mask(size):
    row = lax.broadcasted_iota(jnp.int32, (size, size), 0)
    col = lax.broadcasted_iota(jnp.int32, (size, size), 1)
    return jnp.where(((row ^ col) & (TILE - 1)) == 0, 0.0, LOW)


def pair_cols(part, pair, width):
    start = part * width + pair * PAIR
    return slice(start, start + PAIR)


def temporal_project(x_ref, qk_ref, v_in_ref, v_ref, norm_ref, joined_ref):
    chunk, padded, width = x_ref.shape
    unit, scale = normalize(rows_of(x_ref[...]).astype(F32))
    norm = (unit * v_ref[0:1] + v_ref[1:2]).astype(BF)
    norm_ref[...] = norm.reshape(chunk, padded, width)
    for part in range(3):
        cols = slice(part * width, (part + 1) * width)
        weight = qk_ref[:, cols] if part < 2 else v_in_ref[:, :width]
        joined_ref[:, :, cols] = dot_nn(norm, weight).astype(BF).reshape(chunk, padded, width)


def temporal_attend(joined_ref, mixed_ref):
    frames, tile, width = mixed_ref.shape
    bias = place_mask(frames * tile)
    for first in range(0, PAIRS, GROUP_T):
        group = range(first, first + GROUP_T)
        tiles = [[rows_of(joined_ref[:, :, pair_cols(i, pair, width)]) for i in range(3)] for pair in group]
        for pair, mixed in zip(group, heads_forward(tiles, bias)):
            mixed_ref[:, :, pair_cols(0, pair, width)] = mixed.reshape(frames, tile, PAIR)


def temporal_finish(x_ref, mixed_ref, ol_ref, v_ref, proj_ref, after_ref):
    chunk, padded, width = x_ref.shape
    proj = (dot_nn(rows_of(mixed_ref[...]), ol_ref[:, :width]) + v_ref[2:3]).astype(BF)
    proj_ref[...] = proj.reshape(chunk, padded, width)
    branch = (dot_nn(proj, ol_ref[:, width:]) + v_ref[3:4]).astype(BF)
    after = rows_of(x_ref[...]).astype(F32) + branch.astype(F32)
    after_ref[...] = after.reshape(chunk, padded, width)


def spatial_forward(places, after_ref, s_ref, v_ref, norm_ref, joined_ref, mixed_ref, space_ref):
    chunk, padded, width = after_ref.shape
    after = rows_of(after_ref[...])
    unit, scale = normalize(after)
    norm = (unit * v_ref[4:5] + v_ref[5:6]).astype(BF)
    norm_ref[...] = norm.reshape(chunk, padded, width)
    for part in range(3):
        cols = slice(part * width, (part + 1) * width)
        joined_ref[:, :, cols] = dot_nn(norm, s_ref[:, cols]).astype(BF).reshape(chunk, padded, width)
    allowed = jnp.where(lax.broadcasted_iota(jnp.int32, (1, padded), 1) < places, 0.0, LOW)
    for frame in range(chunk):
        for first in range(0, PAIRS, GROUP_S):
            group = range(first, first + GROUP_S)
            tiles = [[joined_ref[frame, :, pair_cols(i, pair, width)] for i in range(3)] for pair in group]
            for pair, mixed in zip(group, heads_forward(tiles, allowed)):
                mixed_ref[frame, :, pair_cols(0, pair, width)] = mixed
    space = after + dot_nn(rows_of(mixed_ref[...]), s_ref[:, 3 * width :]) + v_ref[6:7]
    space_ref[...] = space.reshape(chunk, padded, width)


def gelu_parts(hidden):
    phi = 0.5 * (1.0 + lax.erf(hidden * 0.7071067811865476))
    density = jnp.exp(-0.5 * hidden * hidden) * 0.3989422804014327
    return phi, density


def feed_both(places, space_ref, cot_ref, w1_ref, w2_ref, v_ref, out_ref, grad_ref, norm_ref, active_ref, dhid_ref, vec_ref):
    chunk, padded, width = space_ref.shape
    blocks = w1_ref.shape[1] // width

    @pl.when(pl.program_id(0) == 0)
    def _():
        vec_ref[...] = jnp.zeros_like(vec_ref)

    space = rows_of(space_ref[...])
    cot = rows_of(cot_ref[...])
    unit, scale = normalize(space)
    norm = (unit * v_ref[7:8] + v_ref[8:9]).astype(BF)
    norm_ref[...] = norm.reshape(chunk, padded, width)
    out = space + v_ref[9:10]
    d_norm = jnp.zeros_like(space)
    for block in range(blocks):
        cols = slice(block * width, (block + 1) * width)
        hidden = dot_nn(norm, w1_ref[:, cols]) + v_ref[10 + block : 11 + block]
        phi, density = gelu_parts(hidden)
        active = (hidden * phi).astype(BF)
        active_ref[:, :, cols] = active.reshape(chunk, padded, width)
        out += dot_nn(active, w2_ref[:, cols])
        d_hidden = dot_nt(cot, w2_ref[:, cols]) * (phi + hidden * density)
        vec_ref[3 + block : 4 + block] += col_sum(d_hidden.astype(BF).astype(F32))
        d_hidden = d_hidden.astype(BF)
        dhid_ref[:, :, cols] = d_hidden.reshape(chunk, padded, width)
        d_norm += dot_nt(d_hidden, w1_ref[:, cols])
    for frame in range(chunk):
        out_ref[frame] = out[frame * padded : frame * padded + places].astype(BF)
    vec_ref[0:1] += col_sum(d_norm * unit)
    vec_ref[1:2] += col_sum(d_norm)
    vec_ref[2:3] += col_sum(cot.astype(F32))
    grad = cot.astype(F32) + norm_back(unit, scale, v_ref[7:8], d_norm)
    grad_ref[...] = grad.reshape(chunk, padded, width)


def feed_grads(norm_ref, dhid_ref, active_ref, cot_ref, out_ref, norm_turned, cot_turned):
    width = norm_ref.shape[1]

    @pl.when(pl.program_id(0) == 0)
    def _():
        norm_turned[...] = norm_ref[...].T
        cot_turned[...] = cot_ref[...].T

    out_ref[:, :width] = dot_nn(norm_turned[...], dhid_ref[...]).astype(BF)
    out_ref[:, width:] = dot_nn(cot_turned[...], active_ref[...]).astype(BF).T


def spatial_back(places, grad_ref, after_ref, joined_ref, s_ref, v_ref, dspace_ref, djoin_ref, dat_ref, dtime_ref, vec_ref, dmix_ref):
    chunk, padded, width = grad_ref.shape

    @pl.when(pl.program_id(0) == 0)
    def _():
        vec_ref[...] = jnp.zeros_like(vec_ref)

    grad = rows_of(grad_ref[...])
    d_space = grad.astype(BF)
    dspace_ref[...] = d_space.reshape(chunk, padded, width)
    vec_ref[2:3] += col_sum(d_space.astype(F32))
    dmix_ref[...] = dot_nt(d_space, s_ref[:, 3 * width :]).astype(BF).reshape(chunk, padded, width)
    allowed = jnp.where(lax.broadcasted_iota(jnp.int32, (padded, 1), 0) < places, 0.0, LOW)
    for frame in range(chunk):
        for first in range(0, PAIRS, GROUP_SB):
            group = range(first, first + GROUP_SB)
            tiles = [
                [joined_ref[frame, :, pair_cols(i, pair, width)] for i in range(3)]
                + [dmix_ref[frame, :, pair_cols(0, pair, width)]]
                for pair in group
            ]
            for pair, grads in zip(group, heads_backward(tiles, allowed)):
                for i in range(3):
                    djoin_ref[frame, :, pair_cols(i, pair, width)] = grads[i]
    d_joined = rows_of(djoin_ref[...])
    d_norm = dot_nt(d_joined, s_ref[:, : 3 * width])
    unit, scale = normalize(rows_of(after_ref[...]))
    vec_ref[0:1] += col_sum(d_norm * unit)
    vec_ref[1:2] += col_sum(d_norm)
    d_time = grad + norm_back(unit, scale, v_ref[4:5], d_norm)
    dat_ref[...] = d_time.reshape(chunk, padded, width)
    dtime_ref[...] = d_time.astype(BF).reshape(chunk, padded, width)


def turned_grads(count, norm_ref, djoin_ref, *refs):
    i = pl.program_id(0)
    out_ref, norm_turned = refs[-2:]

    @pl.when(i == 0)
    def _():
        norm_turned[...] = norm_ref[...].T

    @pl.when(i < count)
    def _():
        out_ref[...] = dot_nn(norm_turned[...], djoin_ref[...]).astype(BF)

    if len(refs) > 2:

        @pl.when(i == count)
        def _():
            out_ref[...] = dot_tn(refs[0][...], refs[1][...]).astype(BF)


def temporal_back_project(dtime_ref, ol_ref, dproj_ref, dmix_ref, vec_ref):
    chunk, padded, width = dtime_ref.shape

    @pl.when(pl.program_id(0) == 0)
    def _():
        vec_ref[...] = jnp.zeros_like(vec_ref)

    d_time = rows_of(dtime_ref[...])
    vec_ref[1:2] += col_sum(d_time.astype(F32))
    d_proj = dot_nt(d_time, ol_ref[:, width:]).astype(BF)
    vec_ref[0:1] += col_sum(d_proj.astype(F32))
    dproj_ref[...] = d_proj.reshape(chunk, padded, width)
    dmix_ref[...] = dot_nt(d_proj, ol_ref[:, :width]).astype(BF).reshape(chunk, padded, width)


def temporal_back_attend(joined_ref, dmix_ref, djoin_ref):
    frames, tile, width = dmix_ref.shape
    bias = place_mask(frames * tile)
    for first in range(0, PAIRS, GROUP_TB):
        group = range(first, first + GROUP_TB)
        tiles = [
            [rows_of(joined_ref[:, :, pair_cols(i, pair, width)]) for i in range(3)]
            + [rows_of(dmix_ref[:, :, pair_cols(0, pair, width)])]
            for pair in group
        ]
        for pair, grads in zip(group, heads_backward(tiles, bias)):
            for i in range(3):
                djoin_ref[:, :, pair_cols(i, pair, width)] = grads[i].reshape(frames, tile, PAIR)


def temporal_back_finish(
    places, me_ref, dat_ref, x_ref, djoin_ref, qk_ref, v_in_ref, v_ref, vec_t_ref, vec_s_ref, vec_f_ref,
    gx_ref, turned_ref, vec_ref,
):
    chunk, padded, width = x_ref.shape

    @pl.when(pl.program_id(0) == 0)
    def _():
        vec_ref[...] = jnp.zeros_like(vec_ref)
        vec_ref[2:4] = vec_t_ref[0:2]
        vec_ref[4:7] = vec_s_ref[0:3]
        vec_ref[7:14] = vec_f_ref[0:7]

    d_joined = rows_of(djoin_ref[...])
    d_norm = dot_nt(d_joined[:, : 2 * width], qk_ref[...]) + dot_nt(d_joined[:, 2 * width :], v_in_ref[:, :width])
    d_norm = d_norm.astype(BF).astype(F32)
    unit, scale = normalize(rows_of(x_ref[...]).astype(F32))
    vec_ref[0:1] += col_sum(d_norm * unit)
    vec_ref[1:2] += col_sum(d_norm)
    grad = rows_of(dat_ref[...]) + norm_back(unit, scale, v_ref[0:1], d_norm)
    gx_ref[...] = grad.astype(BF).reshape(chunk, padded, width)[:, :places]

    @pl.when(pl.program_id(0) == pl.num_programs(0) - 1)
    def _():
        turned_ref[...] = vec_ref[...].T.astype(BF)


def whole(shape):
    return pl.BlockSpec(shape, lambda *i: (0,) * len(shape))


def cost(micros):
    return pl.CostEstimate(flops=int(micros * 1e8), bytes_accessed=0, transcendentals=0)


def params(mib=60):
    return pltpu.CompilerParams(vmem_limit_bytes=mib << 20)


def shape_of(*dims, dtype=BF):
    return jax.ShapeDtypeStruct(dims, dtype)


ANYWHERE = pl.BlockSpec(memory_space=pl.ANY)


def launch(kernel, micros, args, in_specs, out_specs, out_shape, grid, scratch=(), after=()):
    count, skip = len(args), len(after)

    def body(*refs):
        kernel(*refs[:count], *refs[count + skip :])

    return pl.pallas_call(
        body,
        grid=grid,
        in_specs=list(in_specs) + [ANYWHERE] * skip,
        out_specs=out_specs,
        out_shape=out_shape,
        scratch_shapes=list(scratch),
        cost_estimate=cost(micros),
        compiler_params=params(),
    )(*args, *after)


def gate(value, *after):
    return lax.optimization_barrier((value,) + after)[0]


def frame_block(chunk, padded, width):
    return pl.BlockSpec((chunk, padded, width), lambda i: (i, 0, 0))


def place_block(frames, width):
    return pl.BlockSpec((frames, TILE, width), lambda i: (0, i, 0))


def wholes(arrays):
    return [whole(a.shape) for a in arrays]


def flat(a):
    return a.reshape(-1, a.shape[-1])


def run_temporal_project(x, qk, v_in, v, chunk=2, after=()):
    frames, padded, width = x.shape
    block, wide = frame_block(chunk, padded, width), frame_block(chunk, padded, 3 * width)
    return launch(
        temporal_project, 9, (x, qk, v_in, v), [block] + wholes((qk, v_in, v)), [block, wide],
        (shape_of(*x.shape), shape_of(frames, padded, 3 * width)), (frames // chunk,), after=after,
    )


def run_temporal_attend(joined, after=()):
    frames, padded, wide = joined.shape
    width = wide // 3
    return launch(
        temporal_attend, 14, (joined,), [place_block(frames, wide)], place_block(frames, width),
        shape_of(frames, padded, width), (padded // TILE,), after=after,
    )


def run_temporal_finish(x, mixed, ol, v, chunk=2, after=()):
    frames, padded, width = x.shape
    block = frame_block(chunk, padded, width)
    return launch(
        temporal_finish, 8, (x, mixed, ol, v), [block, block] + wholes((ol, v)), [block, block],
        (shape_of(*x.shape), shape_of(*x.shape, dtype=F32)), (frames // chunk,), after=after,
    )


def run_spatial_forward(places, attended, pack, v, chunk=2, after=()):
    frames, padded, width = attended.shape
    block, wide = frame_block(chunk, padded, width), frame_block(chunk, padded, 3 * width)
    dims = attended.shape
    return launch(
        functools.partial(spatial_forward, places), 23, (attended, pack, v),
        [block, pl.BlockSpec((width, 4 * width), lambda i: (0, 2)), whole(v.shape)],
        [block, wide, block, block],
        (shape_of(*dims), shape_of(frames, padded, 3 * width), shape_of(*dims), shape_of(*dims, dtype=F32)),
        (frames // chunk,), after=after,
    )


def run_feed(places, space, cot, pack, v, chunk=2, after=()):
    frames, padded, width = space.shape
    hidden = 4 * width
    block, wide = frame_block(chunk, padded, width), frame_block(chunk, padded, hidden)
    dims = space.shape
    return launch(
        functools.partial(feed_both, places), 45, (space, cot, pack, pack, v),
        [
            block, block,
            pl.BlockSpec((width, hidden), lambda i: (0, 0)),
            pl.BlockSpec((width, hidden), lambda i: (0, 1)),
            whole(v.shape),
        ],
        [frame_block(chunk, places, width), block, block, wide, wide, whole((8, width))],
        (
            shape_of(frames, places, width), shape_of(*dims, dtype=F32), shape_of(*dims),
            shape_of(frames, padded, hidden), shape_of(frames, padded, hidden), shape_of(8, width, dtype=F32),
        ),
        (frames // chunk,), after=after,
    )


def run_feed_grads(norm, d_hidden, active, cot, after=()):
    norm, d_hidden, active, cot = flat(norm), flat(d_hidden), flat(active), flat(cot)
    rows, width = norm.shape
    blocks = d_hidden.shape[1] // width
    part = pl.BlockSpec((rows, width), lambda i: (0, i))
    return launch(
        feed_grads, 25, (norm, d_hidden, active, cot), [whole((rows, width)), part, part, whole((rows, width))],
        pl.BlockSpec((width, 2 * width), lambda i: (0, i)), shape_of(width, 2 * width * blocks), (blocks,),
        scratch=[pltpu.VMEM((width, rows), BF), pltpu.VMEM((width, rows), BF)], after=after,
    )


def run_spatial_back(places, grad, attended, joined, pack, v, chunk=2, after=()):
    frames, padded, width = grad.shape
    block, wide = frame_block(chunk, padded, width), frame_block(chunk, padded, 3 * width)
    dims = grad.shape
    return launch(
        functools.partial(spatial_back, places), 42, (grad, attended, joined, pack, v),
        [block, block, wide, pl.BlockSpec((width, 4 * width), lambda i: (0, 2)), whole(v.shape)],
        [block, wide, block, block, whole((8, width))],
        (
            shape_of(*dims), shape_of(frames, padded, 3 * width), shape_of(*dims, dtype=F32), shape_of(*dims),
            shape_of(8, width, dtype=F32),
        ),
        (frames // chunk,), scratch=[pltpu.VMEM((chunk, padded, width), BF)], after=after,
    )


def run_join_grads(norm, d_joined, *more, after=()):
    norm, d_joined = flat(norm), flat(d_joined)
    more = [flat(a) for a in more]
    rows, width = norm.shape
    count = d_joined.shape[1] // width
    steps = count + (1 if more else 0)
    return launch(
        functools.partial(turned_grads, count), 4 * steps, (norm, d_joined, *more),
        [whole((rows, width)), pl.BlockSpec((rows, width), lambda i: (0, jnp.minimum(i, count - 1)))] + wholes(more),
        pl.BlockSpec((width, width), lambda i: (0, i)), shape_of(width, steps * width), (steps,),
        scratch=[pltpu.VMEM((width, rows), BF)], after=after,
    )


def feed_out(n, g_ref, w1_ref, w2_ref):
    rows, hidden = w1_ref.shape
    width = w2_ref.shape[1]
    parts = hidden // width
    for j in range(parts):
        block = g_ref[:, 2 * j * width : (2 * j + 1) * width].astype(F32)
        for i in range(n):
            at = (i * parts + j) * rows
            w1_ref[:, at : at + rows] = block[:, i * rows : (i + 1) * rows]
        w2_ref[j * rows : (j + 1) * rows] = g_ref[:, (2 * j + 1) * width : (2 * j + 2) * width].astype(F32)


def run_feed_out(g, n):
    rows = g.shape[0]
    width = rows * n
    parts = g.shape[1] // (2 * width)
    outs = (shape_of(rows, parts * width, dtype=F32), shape_of(parts * rows, width, dtype=F32))
    return pl.pallas_call(
        functools.partial(feed_out, n), out_shape=outs, cost_estimate=cost(3), compiler_params=params()
    )(g)


def tile_grad(a_ref, b_ref, out_ref):
    out_ref[...] = dot_tn(a_ref[...], b_ref[...]).astype(BF)


def run_tile_grad(a, b, after=()):
    a, b = flat(a), flat(b)
    rows, width = a.shape
    return launch(
        tile_grad, 6, (a, b), [pl.BlockSpec((rows, width // 2), lambda i: (0, i)), whole(b.shape)],
        pl.BlockSpec((width // 2, b.shape[1]), lambda i: (i, 0)), shape_of(width, b.shape[1]), (2,), after=after,
    )


def run_temporal_back_project(d_time, ol, chunk=2, after=()):
    frames, padded, width = d_time.shape
    block = frame_block(chunk, padded, width)
    dims = d_time.shape
    return launch(
        temporal_back_project, 8, (d_time, ol), [block, whole(ol.shape)], [block, block, whole((8, width))],
        (shape_of(*dims), shape_of(*dims), shape_of(8, width, dtype=F32)), (frames // chunk,), after=after,
    )


def run_temporal_back_attend(joined, d_mixed, after=()):
    frames, padded, width = d_mixed.shape
    wide = place_block(frames, 3 * width)
    return launch(
        temporal_back_attend, 20, (joined, d_mixed), [wide, place_block(frames, width)], wide,
        shape_of(frames, padded, 3 * width), (padded // TILE,), after=after,
    )


def run_temporal_back_finish(places, chunk, me, d_at, x, d_joined, qk, v_in, v, vecs, after=()):
    frames, padded, width = x.shape
    skip = len(after)

    def body(*refs):
        temporal_back_finish(places, *refs[:10], *refs[10 + skip :])

    def mixed_block(height, wide):
        return pl.BlockSpec((chunk, height, wide), lambda i, me: (jnp.bitwise_xor(i, me[0]), 0, 0))

    consts = (qk, v_in, v) + tuple(vecs)
    return pl.pallas_call(
        body,
        grid_spec=pltpu.PrefetchScalarGridSpec(
            num_scalar_prefetch=1,
            grid=(frames // chunk,),
            in_specs=[mixed_block(padded, width), mixed_block(padded, width), mixed_block(padded, 3 * width)]
            + wholes(consts) + [ANYWHERE] * skip,
            out_specs=[pl.BlockSpec((chunk, places, width), lambda i, me: (i, 0, 0)), whole((width, PAIR))],
            scratch_shapes=[pltpu.VMEM((PAIR, width), F32)],
        ),
        out_shape=(shape_of(frames, places, width), shape_of(width, PAIR)),
        cost_estimate=cost(13),
        compiler_params=params(),
    )(me, d_at, x, d_joined, *consts, *after)


AXES = ("dp_hi", "dp_lo", "seq_hi", "seq_lo")
SEQ = AXES[2:]


def swap(values, bit, n):
    return lax.ppermute(values, AXES, [(i, i ^ (1 << bit)) for i in range(n)])


class Gather:
    def __init__(self, values, n, order):
        self.n, self.bits, self.order = n, n.bit_length() - 1, list(order)
        self.me = lax.axis_index(AXES)
        self.tail = values.shape[1:]
        self.held = values.reshape((1,) * self.bits + values.shape)

    def start(self):
        self.bit = self.order.pop(0)
        self.got = swap(self.held, self.bit, self.n)
        return self.held

    def end(self, *after):
        got = gate(self.got, *after) if after else self.got
        axis = self.bits - 1 - self.bit
        high = ((self.me >> self.bit) & 1) == 1
        held = self.held
        self.held = jnp.concatenate([jnp.where(high, got, held), jnp.where(high, held, got)], axis)

    def steps(self, count):
        for _ in range(count):
            self.start()
            self.end()

    def rest(self):
        self.steps(len(self.order))
        return self.result()

    def result(self):
        return self.held.reshape((-1,) + self.tail)


class Scatter:
    def __init__(self, values, n, order, axes):
        self.n, self.bits, self.order, self.axes = n, n.bit_length() - 1, list(order), axes
        self.rows, self.tail = values.shape[0] // n, values.shape[1:]
        self.me = lax.axis_index(AXES)
        self.held = values.reshape((2,) * self.bits + (self.rows,) + self.tail)

    def start(self):
        self.last = not self.order
        if self.last and self.axes:
            held = self.held.reshape((-1, self.rows) + self.tail)
            self.got = lax.all_to_all(held, self.axes, split_axis=0, concat_axis=0, tiled=True)
            return held
        bit = self.order.pop(0)
        axis = self.bits - 1 - bit
        mine = (self.me >> bit) & 1
        send = lax.dynamic_index_in_dim(self.held, 1 - mine, axis, keepdims=True)
        self.keep = lax.dynamic_index_in_dim(self.held, mine, axis, keepdims=True)
        self.got = swap(send, bit, self.n)
        return send

    def end(self, *after):
        got = gate(self.got, *after) if after else self.got
        if self.last:
            self.held = jnp.sum(got.astype(F32), axis=0)
        else:
            self.held = (self.keep.astype(F32) + got.astype(F32)).astype(self.held.dtype)

    def rest(self, *after):
        while self.order:
            self.start()
            self.end()
        if self.axes:
            self.start()
            self.end(*after)
        return self.held.astype(F32).reshape((self.rows,) + self.tail)


def on_device(n, tokens, tg, tb, t_in, t_out, t_lin, sg, sb, s_in, s_out, fg, fb, w1, b1, w2, cotangent):
    bits = n.bit_length() - 1
    top = tuple(range(bits - 1, 2, -1))
    order_a, order_b, order_c = top + (1, 2, 0), top + (2, 1, 0), (2,) + top + (1, 0)
    with_y, with_x = ((0, 2), (AXES[0], AXES[2])), ((0, 1), AXES[:2])
    rows, width = t_in.shape[0], t_in.shape[0] * n
    parts = w2.shape[0] // rows
    hidden = w1.shape[1]
    places = tokens.shape[2]
    frames = tokens.shape[0] * tokens.shape[1]
    extra = -places % TILE

    vecs = jnp.concatenate([tg[None], tb, sg[None], sb, fg[None], fb, b1.reshape(parts, rows)], axis=0)
    n_vec = vecs.shape[0]
    vec_cols = jnp.pad(vecs.T, ((0, 0), (0, 2 * HEAD_DIM - n_vec)))
    feed = jnp.concatenate(
        [
            w1.reshape(rows, n, parts, rows).transpose(0, 2, 1, 3).reshape(rows, hidden),
            w2.reshape(parts, rows, width).transpose(1, 0, 2).reshape(rows, hidden),
            s_in,
            s_out,
        ],
        axis=1,
    )
    feed = lax.all_gather(feed, AXES, axis=0, tiled=True)

    def own_clip(grid):
        clip = lax.all_to_all(grid, SEQ, split_axis=0, concat_axis=0, tiled=True)
        return jnp.pad(clip.reshape(frames, places, width), ((0, 0), (0, extra), (0, 0)))

    def own_frames(clip):
        return lax.all_to_all(clip.reshape(tokens.shape), SEQ, split_axis=0, concat_axis=0, tiled=True)

    def swap_pieces(clip, count):
        pieces = clip.reshape((count, tokens.shape[1]) + tokens.shape[2:])
        return [pieces[0]] + [lax.ppermute(pieces[k], AXES, [(i, i ^ k) for i in range(n)]) for k in range(1, count)]

    def in_order(got, me):
        step = 1
        while step < len(got):
            flip = (me & step) != 0
            got = [jnp.where(flip, got[j ^ step], got[j]) for j in range(len(got))]
            step *= 2
        return jnp.stack(got)

    x = own_clip(tokens)
    t_qk = Gather(t_in[:, : 2 * width], n, order_a)
    t_v = Gather(jnp.concatenate([t_in[:, 2 * width :], vec_cols], axis=1), n, order_c)
    t_ol = Gather(jnp.concatenate([t_out, t_lin], axis=1), n, order_b)
    t_qk_w, t_v_w = t_qk.rest(), t_v.rest()
    t_ol.steps(bits - 1)
    vec = t_v_w[:, width:].T[:16].astype(F32)
    norm_t, joined_t = run_temporal_project(x, t_qk_w, t_v_w, vec, after=(t_ol.start(),))
    t_ol.end(norm_t)
    t_ol_w = t_ol.result()
    mixed_t = run_temporal_attend(joined_t)
    proj_t, after_time = run_temporal_finish(x, mixed_t, t_ol_w, vec)
    cot = own_clip(gate(cotangent, norm_t))
    norm_s, joined_s, mixed_s, after_space = run_spatial_forward(places, after_time, feed, vec)
    out, d_after_space, norm_m, active, d_hidden, vec_f = run_feed(places, after_space, cot, feed, vec)
    output = own_frames(out)
    g_feed_all = run_feed_grads(norm_m, d_hidden, active, cot)
    g_feed = lax.psum_scatter(g_feed_all, AXES, scatter_dimension=0, tiled=True)
    o_w1, o_w2 = run_feed_out(g_feed, n)
    d_space, d_joined_s, d_after_time, d_time, vec_s = run_spatial_back(
        places, d_after_space, after_time, joined_s, feed, vec, after=(g_feed_all,)
    )
    g_space = run_join_grads(norm_s, d_joined_s, mixed_s, d_space, after=(output[0, :1, 0, :128],))

    def beside(chains, kernel, *args, after=()):
        sends = tuple(chain.start() for chain in chains)
        done = kernel(*args, after=sends + tuple(after))
        for chain in chains:
            chain.end(done[0] if isinstance(done, (tuple, list)) else done)
        return done

    gs = Scatter(g_space, n, *with_y)
    g_lin = beside((gs,), run_tile_grad, proj_t, d_time)
    sends = (gs.start(),)
    d_proj, d_mixed_t, vec_t1 = run_temporal_back_project(d_time, t_ol_w, after=sends)
    g_out = run_tile_grad(mixed_t, d_proj, after=sends)
    go = Scatter(jnp.concatenate([g_out, g_lin], axis=1), n, (0, 1, 2) + top[::-1], None)
    d_joined_t = beside((go,), run_temporal_back_attend, joined_t, d_mixed_t)
    gs.end(d_joined_t)
    sends = (gs.start(),)
    g_qkv = beside((go,), run_join_grads, norm_t, d_joined_t)
    half = 3 * width // 2
    gq = Scatter(g_qkv[:, :half], n, (0,), (AXES[0], AXES[1], AXES[2]))
    gq.start()
    me_seq = (lax.axis_index(SEQ)).astype(jnp.int32)
    g_x, vec_cols = beside(
        (go,), run_temporal_back_finish, places, tokens.shape[1], me_seq.reshape(1), d_after_time, x, d_joined_t,
        t_qk_w, t_v_w, vec, (vec_t1, vec_s, vec_f),
    )
    gs.end(g_x)
    gq.end(g_x, o_w1)
    gr = Scatter(jnp.concatenate([g_qkv[:, half:], gate(vec_cols, gq.held)], axis=1), n, *with_y)
    pieces = swap_pieces(g_x, tokens.shape[0])
    for after in ((), pieces[1:]):
        gr.start()
        gr.end(*after)
    g_q = gq.rest()
    g_x = in_order(pieces, me_seq)
    g_o = go.rest()
    g_r = gr.rest()
    g_s = gs.held.reshape(rows, 4 * width)
    g_i = jnp.concatenate([g_q, g_r[:, :half]], axis=1)
    v = g_r[:, half : half + n_vec].T
    return (
        output, g_x, v[0], v[1:4], g_i, g_o[:, :width], g_o[:, width : 2 * width],
        v[4], v[5:7], g_s[:, : 3 * width], g_s[:, 3 * width :], v[7], v[8:10],
        o_w1, v[10 : 10 + parts].reshape(-1), o_w2,
    )


def solution(mesh):
    dp, seq = AXES[:2], AXES[2:]
    dims = mesh.devices.shape
    halved = jax.sharding.Mesh(mesh.devices.reshape(dims[0] // 2, 2, dims[1] // 2, 2), AXES)
    shard = P(AXES)
    cols = P(None, AXES)
    mat = P(AXES, None)
    tok = P(dp, seq, None, None)
    in_specs = (tok, shard, cols, mat, mat, mat, shard, cols, mat, mat, shard, cols, mat, shard, mat, tok)
    out_specs = (tok, tok, shard, cols, mat, mat, mat, shard, cols, mat, mat, shard, cols, mat, shard, mat)
    return jax.shard_map(
        functools.partial(on_device, mesh.size), mesh=halved, in_specs=in_specs, out_specs=out_specs, check_vma=False
    )
```
